32 devices in a mesh: ctx: 8 (over z, y), tp: 4 (over x, core).
Axes of the slice: x: 2, y: 2, z: 4, core: 2. Of those that a mesh axis runs over, the one named last changes fastest.
Arguments:
- queries: bfloat16 [1024, 12288], P('ctx', 'tp'), may hold values from -8 to 8
- keys: bfloat16 [1024, 1024], P('ctx'), may hold values from -16 to 16
- values: bfloat16 [1024, 1024], P('ctx'), may hold values from -6 to 6
- doc_ids: int32 [1024], replicated, may hold values from 0 to 3, never falling along the last dimension, each value on 1 to 640 neighbouring positions
- replica_of: int32 [4], replicated, may hold values from 0 to 7, as said below
- step_query: bfloat16 [4, 12288], P(None, 'tp'), may hold values from -8 to 8
- step_key: bfloat16 [4, 1024], replicated, may hold values from -16 to 16
- step_value: bfloat16 [4, 1024], replicated, may hold values from -6 to 6
- out_weight: bfloat16 [12288, 12288], P('tp', 'ctx'), may hold values from -0.0546875 to 0.0546875
Outputs:
- context: bfloat16 [1024, 12288], P('ctx', 'tp')
- next_hidden: bfloat16 [8, 12288], P(None, 'ctx')
- replica_keys: bfloat16 [8, 1024, 640], P('ctx', 'tp')
- replica_values: bfloat16 [8, 1024, 640], P('ctx', 'tp')
The draws below stay inside these ranges and needn't reach their ends.
Inputs may be any that keep to these rules, and one draw needn't show every extreme that they name: `doc_ids`: documents occupy whole runs of positions in rising order; each has 1 to 640 positions, and one has exactly 640. `replica_of`: the documents name distinct replicas.
All inputs are finite; a program needn't handle non-finite values.
Results may differ from the reference program's by a relative error of at most 0.02.
Values may be sent and summed in bfloat16 or wider, within the bound.
A program may use at most 64 MiB of HBM per device.

```python
import math
import jax
import jax.numpy as jnp
import numpy as np
from jax import lax

D = 12288
H = 96
KVH = 8
HD = 128
NDOC = 4
TOKENS = 1024
MOST = 640
N_CTX = 8


def draw_queries(key, part):
    key = jax.random.fold_in(key, 11)
    result = jnp.clip(jax.random.normal(key, (TOKENS, D), jnp.float32), -6.0, 6.0)
    return result.astype(jnp.bfloat16)


def draw_keys(key, part):
    key = jax.random.fold_in(key, 12)
    result = jnp.clip(3.0 * jax.random.normal(key, (TOKENS, KVH * HD), jnp.float32), -15.0, 15.0)
    return result.astype(jnp.bfloat16)


def draw_step_query(key, part):
    key = jax.random.fold_in(key, 13)
    result = jnp.clip(jax.random.normal(key, (NDOC, D), jnp.float32), -6.0, 6.0)
    return result.astype(jnp.bfloat16)


def draw_replica_of(key, part):
    key = jax.random.fold_in(key, 14)
    first_key, second_key = jax.random.split(key)
    shuffled = jax.random.permutation(first_key, N_CTX).astype(jnp.int32)
    last_slot = jnp.argmax(shuffled == N_CTX - 1).astype(jnp.int32)
    shift_by = jax.random.randint(second_key, (), 0, NDOC, dtype=jnp.int32)
    return jnp.roll(shuffled, shift_by - last_slot)[:NDOC].astype(jnp.int32)


def steps_of(key, dims, cuts, smallest, largest):
    gain, own = 1.0, jax.random.fold_in(key, 6)
    for dim, blocks in cuts:
        heights = jnp.exp(jax.random.uniform(jax.random.fold_in(own, dim), (blocks,), jnp.float32, smallest / len(cuts), largest / len(cuts)))
        gain = gain * jnp.repeat(heights, dims[dim] // blocks).reshape([-1 if axis == dim else 1 for axis in range(len(dims))])
    return gain


def length_profile(number_of, total, reach, skew):
    weights = [(1 << 20) // math.isqrt(standing ** skew) + 1 for standing in range(2, number_of + 1)]
    rest, given = total - reach - (number_of - 1), [1] * (number_of - 1)
    while rest > 0:
        candidates = [i for i in range(number_of - 1) if given[i] < reach]
        pool, left = sum([weights[i] for i in candidates]), rest
        for i in candidates:
            more = min(reach - given[i], max(1, left * weights[i] // pool), rest)
            given[i] = given[i] + more
            rest = rest - more
    return np.array([reach] + given)


def ragged_sizes(key, number_of, total, limit, lean):
    if number_of == 2:
        one = jax.random.randint(key, (), max(1, total - limit), min(limit, total - 1) + 1)
        return jnp.stack([one, total - one])
    tallies = jnp.asarray(length_profile(number_of, total, limit, lean), jnp.int32)
    pairs = (number_of - 1) // 2
    giver, taker = tallies[1:1 + 2 * pairs:2], tallies[2:2 + 2 * pairs:2]
    margin = jnp.minimum(giver - 1, limit - taker)
    shifted = jax.random.randint(jax.random.fold_in(key, 1), (pairs,), 0, 1 << 20) % (margin + 1)
    tallies = tallies.at[1:1 + 2 * pairs:2].set(giver - shifted).at[2:2 + 2 * pairs:2].set(taker + shifted)
    return tallies[jax.random.permutation(jax.random.fold_in(key, 2), number_of)]


def scatter_about(rng, shape, width, reach, shards=(), kind=jnp.bfloat16):
    values = jax.random.normal(rng, shape, jnp.float32) * width
    if len(shards) > 0:
        values = steps_of(rng, shape, shards, -0.22, 0.18) * values
    return jnp.clip(values, min=-reach, max=reach).astype(kind)


def setup_inputs(seed: int = 0) -> dict:
    key_of = jax.random.split(jax.random.key(seed), 10)
    queries = draw_queries(jax.random.fold_in(key_of[9], 71), 0)
    keys = draw_keys(jax.random.fold_in(key_of[9], 71), 0)
    values = scatter_about(key_of[2], (TOKENS, KVH * HD), 1.0, 6.0, ((0, 8),))
    doc_ids = jnp.searchsorted(jnp.cumsum(ragged_sizes(key_of[3], NDOC, TOKENS, MOST, 0)), jnp.arange(TOKENS), side="right").astype(jnp.int32)
    replica_of = draw_replica_of(jax.random.fold_in(key_of[9], 71), 0)
    step_query = draw_step_query(jax.random.fold_in(key_of[9], 71), 0)
    step_key = scatter_about(key_of[6], (NDOC, KVH * HD), 4.0, 16.0)
    step_value = scatter_about(key_of[7], (NDOC, KVH * HD), 1.0, 6.0)
    out_weight = scatter_about(key_of[8], (D, D), D ** -0.5, 0.0546875, ((0, 4), (1, 8)))
    return {"queries": queries, "keys": keys, "values": values, "doc_ids": doc_ids, "replica_of": replica_of, "step_query": step_query, "step_key": step_key, "step_value": step_value, "out_weight": out_weight}


def reference(queries, keys, values, doc_ids, replica_of, step_query, step_key, step_value, out_weight):
    group_size = H // KVH
    score_scale = 1.0 / math.sqrt(HD)
    block_rows = 64
    highest = lax.Precision.HIGHEST
    keys_wide = keys.astype(jnp.float32).reshape(TOKENS, KVH, HD)
    values_wide = values.astype(jnp.float32).reshape(TOKENS, KVH, HD)
    positions = jnp.arange(TOKENS, dtype=jnp.int32)

    def one_block(start):
        query_block = lax.dynamic_slice_in_dim(queries, start, block_rows, 0).astype(jnp.float32)
        query_block = query_block.reshape(block_rows, KVH, group_size, HD)
        query_pos = start + jnp.arange(block_rows, dtype=jnp.int32)
        query_doc = lax.dynamic_slice_in_dim(doc_ids, start, block_rows, 0)
        scores = jnp.einsum('bkgd,lkd->kgbl', query_block, keys_wide, precision=highest) * score_scale
        allowed = (doc_ids[None, :] == query_doc[:, None]) & (positions[None, :] <= query_pos[:, None])
        masked = jnp.where(allowed[None, None], scores, -1e+30)
        row_top = lax.optimization_barrier(jnp.max(masked, axis=-1))
        weights = jnp.where(allowed[None, None], jnp.exp(scores - row_top[..., None]), 0.0)
        row_total = lax.optimization_barrier(jnp.sum(weights, axis=-1))
        rounded = lax.optimization_barrier(weights.astype(jnp.bfloat16)).astype(jnp.float32)
        summed = jnp.einsum('kgbl,lkd->bkgd', rounded, values_wide, precision=highest)
        summed = summed / jnp.transpose(row_total, (2, 0, 1))[..., None]
        return summed.reshape(block_rows, D).astype(jnp.bfloat16)
    block_starts = jnp.arange(0, TOKENS, block_rows, dtype=jnp.int32)
    block_outs = lax.map(one_block, block_starts)
    context = block_outs.reshape(TOKENS, D)

    def one_doc(doc_index):
        inside = doc_ids == doc_index
        query_row = step_query[doc_index].astype(jnp.float32).reshape(KVH, group_size, HD)
        own_key = step_key[doc_index].astype(jnp.float32).reshape(KVH, HD)
        own_value = step_value[doc_index].astype(jnp.float32).reshape(KVH, HD)
        cached = jnp.einsum('kgd,lkd->kgl', query_row, keys_wide, precision=highest) * score_scale
        own_score = jnp.einsum('kgd,kd->kg', query_row, own_key, precision=highest) * score_scale
        row_top = jnp.maximum(lax.optimization_barrier(jnp.max(jnp.where(inside[None, None], cached, -1e+30), axis=-1)), own_score)
        weights = jnp.where(inside[None, None], jnp.exp(cached - row_top[..., None]), 0.0)
        own_prob = jnp.exp(own_score - row_top)
        row_total = lax.optimization_barrier(jnp.sum(weights, axis=-1)) + own_prob
        rounded = lax.optimization_barrier(weights.astype(jnp.bfloat16)).astype(jnp.float32)
        own_rounded = lax.optimization_barrier(own_prob.astype(jnp.bfloat16)).astype(jnp.float32)
        summed = jnp.einsum('kgl,lkd->kgd', rounded, values_wide, precision=highest)
        summed = summed + own_rounded[..., None] * own_value[:, None, :]
        return (summed / row_total[..., None]).reshape(D).astype(jnp.bfloat16)
    attended = lax.map(one_doc, jnp.arange(NDOC, dtype=jnp.int32))
    replica_hot = (replica_of[None, :] == jnp.arange(N_CTX, dtype=jnp.int32)[:, None]).astype(jnp.float32)
    placed = jnp.dot(replica_hot, attended.astype(jnp.float32), precision=highest).astype(jnp.bfloat16)
    next_hidden = jnp.dot(placed, out_weight, preferred_element_type=jnp.float32).astype(jnp.bfloat16)
    doc_numbers = jnp.arange(NDOC, dtype=jnp.int32)

    def one_replica(replica):
        match_rows = (replica_of == replica).astype(jnp.int32)
        has_request = jnp.sum(match_rows) > 0
        chosen_doc = jnp.sum(match_rows * doc_numbers)
        doc_start = jnp.sum((doc_ids < chosen_doc).astype(jnp.int32))
        doc_length = jnp.sum((doc_ids == chosen_doc).astype(jnp.int32))
        slots = jnp.arange(MOST, dtype=jnp.int32)
        live = (slots < doc_length) & has_request
        source_rows = jnp.clip(doc_start + slots, 0, TOKENS - 1).astype(jnp.int32)
        slot_keys = jnp.where(live[:, None], jnp.take(keys, source_rows, axis=0), jnp.zeros((), keys.dtype))
        slot_values = jnp.where(live[:, None], jnp.take(values, source_rows, axis=0), jnp.zeros((), values.dtype))
        return (jnp.transpose(slot_keys, (1, 0)), jnp.transpose(slot_values, (1, 0)))
    replica_keys, replica_values = lax.map(one_replica, jnp.arange(N_CTX, dtype=jnp.int32))
    return (context, next_hidden, replica_keys, replica_values)
```

```python
import functools
import math

import jax
import jax.numpy as jnp
from jax import lax
from jax.experimental import pallas as pl
from jax.experimental.pallas import tpu as pltpu
from jax.sharding import PartitionSpec as P

H = 96
KVH = 8
HD = 128
PER = H // KVH
MESH = pl.DeviceIdType.MESH
EXP_SCALE = math.log2(math.e) / math.sqrt(HD)
F32 = jnp.float32
BF16 = jnp.bfloat16
NT = (((1,), (1,)), ((), ()))
NN = (((1,), (0,)), ((), ()))
TN = (((0,), (0,)), ((), ()))


def dot(a, b, dims):
    return lax.dot_general(a, b, dims, preferred_element_type=F32)


def kernel(
    n, ntp, heads, kv_dev,
    q_hbm, k_hbm, v_hbm, doc_ref, rep_ref, sq_ref, sk_ref, sv_ref, w_hbm,
    ctx_ref, next_ref, rk_ref, rv_ref,
    kbuf, vbuf, qbuf, wbuf, acc, tops, bias, dstart, sq_scr, sk_scr, sv_scr, att, pack, cut, out_buf, in_buf,
    local_sem, send_sem, recv_sem, part_send, part_recv,
):
    me = lax.axis_index("ctx")
    tp = lax.axis_index("tp")
    half = n // 2
    line = me // 2
    side = me % 2
    mate = 2 * line + 1 - side
    rows = kbuf.shape[1]
    width = kbuf.shape[2]
    per = heads // kv_dev
    first_kv = tp * heads // PER
    tokens = n * rows
    ndoc = sq_ref.shape[0]

    columns = pl.ds(pl.multiple_of(first_kv * HD, HD), width)
    k_copy = pltpu.make_async_copy(k_hbm.at[:, columns], kbuf.at[me], local_sem.at[0])
    v_copy = pltpu.make_async_copy(v_hbm.at[:, columns], vbuf.at[me], local_sem.at[1])
    q_copy = pltpu.make_async_copy(q_hbm, qbuf, local_sem.at[2])
    w_copy = pltpu.make_async_copy(w_hbm, wbuf, local_sem.at[3])
    k_copy.start()
    v_copy.start()
    q_copy.start()
    w_copy.start()

    barrier = pltpu.get_barrier_semaphore()
    pl.semaphore_signal(barrier, inc=1, device_id={"ctx": mate}, device_id_type=MESH)
    for t in range(1, ntp):
        pl.semaphore_signal(barrier, inc=1, device_id={"tp": lax.rem(tp + t, ntp)}, device_id_type=MESH)

    @pl.when(line > 0)
    def _():
        pl.semaphore_signal(barrier, inc=1, device_id={"ctx": me - 2}, device_id_type=MESH)

    @pl.when(line < half - 1)
    def _():
        pl.semaphore_signal(barrier, inc=1, device_id={"ctx": me + 2}, device_id_type=MESH)

    docs = doc_ref[...].astype(F32)
    starts = [jnp.sum(jnp.where(docs < d, 1.0, 0.0), axis=1, keepdims=True) for d in range(ndoc + 1)]
    own_docs = doc_ref[:, pl.ds(pl.multiple_of(me * rows, rows), rows)].astype(F32)
    begin = jnp.zeros_like(own_docs)
    for d in range(1, ndoc):
        begin = jnp.where(own_docs == d, starts[d], begin)
    dstart[...] = jnp.transpose(jnp.broadcast_to(begin, (rows, rows)))
    sq_scr[...] = jnp.zeros_like(sq_scr)
    sk_scr[...] = jnp.zeros_like(sk_scr)
    sv_scr[...] = jnp.zeros_like(sv_scr)
    sq = sq_ref[...].astype(F32)
    for h in range(heads):
        sq_scr[h, 0:ndoc, :] = sq[:, h * HD:(h + 1) * HD]
    for g in range(kv_dev):
        head_columns = pl.ds(pl.multiple_of((first_kv + g) * HD, HD), HD)
        sk_scr[g, 0:ndoc, :] = sk_ref[:, head_columns].astype(F32)
        sv_scr[g, 0:ndoc, :] = sv_ref[:, head_columns].astype(F32)
    tops[...] = jnp.full(tops.shape, -1e30, F32)
    acc[...] = jnp.zeros(acc.shape, F32)

    k_copy.wait()
    v_copy.wait()
    q_copy.wait()
    neighbours = 1 + (ntp - 1) + jnp.where(line > 0, 1, 0) + jnp.where(line < half - 1, 1, 0)
    pl.semaphore_wait(barrier, neighbours)

    def move(way, owner, piece):
        buf = (kbuf, vbuf)[piece]
        target = (me + 2, me - 2, mate)[way]
        return pltpu.make_async_remote_copy(
            src_ref=buf.at[owner],
            dst_ref=buf.at[owner],
            send_sem=send_sem.at[way, owner, piece],
            recv_sem=recv_sem.at[owner, piece],
            device_id={"ctx": target},
            device_id_type=MESH,
        )

    for piece in range(2):
        @pl.when(line < half - 1)
        def _():
            move(0, me, piece).start()

        @pl.when(line > 0)
        def _():
            move(1, me, piece).start()

        move(2, me, piece).start()

    def group(o):
        j = 2 * o * rows + lax.broadcasted_iota(jnp.int32, (rows, 2 * rows), 1)
        i = me * rows + lax.broadcasted_iota(jnp.int32, (rows, 2 * rows), 0)
        seen = (j <= i) & (j.astype(F32) >= jnp.concatenate([dstart[...]] * 2, axis=1))
        bias[...] = jnp.where(seen, 0.0, -1e30)
        for g in range(kv_dev):
            lanes = slice(g * HD, (g + 1) * HD)
            k = kbuf[pl.ds(2 * o, 2), :, lanes].reshape(2 * rows, HD)
            v = vbuf[pl.ds(2 * o, 2), :, lanes].reshape(2 * rows, HD)
            v = jnp.concatenate([v, jnp.ones_like(v)], axis=1)

            def some_heads(t, carry, g=g, k=k, v=v):
                for u in range(3):
                    h = g * per + t * 3 + u
                    q = qbuf[:, pl.ds(pl.multiple_of(h * HD, HD), HD)]
                    s = dot(q, k, NT) + bias[...]
                    old = tops[h]
                    top = jnp.maximum(old, jnp.max(s, axis=1, keepdims=True))
                    weights = jnp.exp2((s - jnp.concatenate([top, top], axis=1)) * EXP_SCALE)
                    fade = jnp.exp2((old - top) * EXP_SCALE)
                    tops[h] = top
                    acc[h] = acc[h] * jnp.concatenate([fade, fade], axis=1) + dot(weights.astype(BF16), v, NN)
                return carry

            lax.fori_loop(0, per // 3, some_heads, 0)

    back = 5 * n // 8

    def step(s, carry):
        low = line - s
        high = line + s
        for piece in range(2):
            @pl.when(low >= 0)
            def _():
                owner = 2 * low + side
                move(0, owner, piece).wait_recv()

                @pl.when(line < half - 1)
                def _():
                    move(0, owner, piece).start()

                move(2, owner, piece).start()

            @pl.when(high < half)
            def _():
                owner = 2 * high + side
                move(1, owner, piece).wait_recv()

                @pl.when(line > 0)
                def _():
                    move(1, owner, piece).start()

                move(2, owner, piece).start()
        low = line - (s - 1)
        high = line + (s - 1)

        @pl.when(low >= 0)
        def _():
            for piece in range(2):
                move(2, 2 * low + 1 - side, piece).wait_recv()

        @pl.when((high < half) & (s > 1))
        def _():
            for piece in range(2):
                move(2, 2 * high + 1 - side, piece).wait_recv()

        @pl.when((low >= 0) & (2 * low + 1 >= me - back))
        def _():
            group(low)

        return carry

    lax.fori_loop(1, half + 1, step, 0)

    shape = (per * 8, tokens)
    row_doc = (lax.broadcasted_iota(jnp.int32, shape, 0) % 8).astype(F32)
    inside = row_doc == docs
    for g in range(kv_dev):
        lanes = slice(g * HD, (g + 1) * HD)
        k = kbuf[:, :, lanes].reshape(tokens, HD)
        v = vbuf[:, :, lanes].reshape(tokens, HD)
        q = sq_scr[g * per:(g + 1) * per]
        own = jnp.sum(q * sk_scr[g][None], axis=2, keepdims=True).reshape(per * 8, 1)
        s = dot(q.reshape(per * 8, HD).astype(BF16), k, NT)
        top = jnp.maximum(jnp.max(jnp.where(inside, s, -1e30), axis=1, keepdims=True), own)
        weights = jnp.where(inside, jnp.exp2((s - top) * EXP_SCALE), 0.0)
        own_weight = jnp.exp2((own - top) * EXP_SCALE)
        total = jnp.sum(weights, axis=1, keepdims=True) + own_weight
        own_value = jnp.broadcast_to(sv_scr[g][None], (per, 8, HD)).reshape(per * 8, HD)
        mixed = dot(weights.astype(BF16), v, NN) + own_weight.astype(BF16).astype(F32) * own_value
        mixed = mixed / total
        for u in range(per):
            h = g * per + u
            att[0:8, h * HD:(h + 1) * HD] = mixed[u * 8:(u + 1) * 8]
    att[8:16, :] = jnp.zeros((8, heads * HD), F32)

    w_copy.wait()
    pieces = cut.shape[0]
    size = cut.shape[2]
    rows_in = att[...].astype(BF16)
    for c in range(pieces):
        cut[c] = dot(rows_in, wbuf[:, c * size:(c + 1) * size], NN)[0:8]
    pack[...] = jnp.zeros_like(pack)
    for c in range(pieces):
        pack[c * ndoc:(c + 1) * ndoc, :] = cut[c, 0:ndoc, :]
    out_buf[...] = pack[...].astype(BF16)
    sends = []
    for t in range(1, ntp):
        sends.append(pltpu.make_async_remote_copy(
            src_ref=out_buf,
            dst_ref=in_buf.at[t],
            send_sem=part_send.at[t],
            recv_sem=part_recv.at[t],
            device_id={"tp": lax.rem(tp + t, ntp)},
            device_id_type=MESH,
        ))
    for copy in sends:
        copy.start()

    for h in range(heads):
        ctx_ref[:, h * HD:(h + 1) * HD] = (acc[h, :, 0:HD] / acc[h, :, HD:2 * HD]).astype(BF16)

    start = jnp.zeros((1, 1), F32)
    length = jnp.zeros((1, 1), F32)
    for d in range(ndoc):
        named = rep_ref[d] == me
        start = jnp.where(named, starts[d], start)
        length = jnp.where(named, starts[d + 1] - starts[d], length)
    slots = rk_ref.shape[2]
    out_rows = rk_ref.shape[1]
    chunk = slots // max(1, tokens // 1024)
    for first in range(0, slots, chunk):
        slot = (first + lax.broadcasted_iota(jnp.int32, (1, chunk), 1)).astype(F32)
        source = jnp.where(slot < length, slot + start, -1.0)
        position = lax.broadcasted_iota(jnp.int32, (tokens, chunk), 0).astype(F32)
        pick = jnp.where(position == source, 1.0, 0.0).astype(BF16)
        for buf, ref in ((kbuf, rk_ref), (vbuf, rv_ref)):
            taken = dot(buf[...].reshape(tokens, width), pick, TN).astype(BF16)
            if out_rows < width:
                taken = jnp.where(tp % (width // out_rows) == 0, taken[0:out_rows], taken[out_rows:2 * out_rows])
            ref[0, :, first:first + chunk] = taken

    summed = out_buf[...].astype(F32)
    for t in range(1, ntp):
        sends[t - 1].wait_recv()
        summed = summed + in_buf[t].astype(F32)
    replica = lax.broadcasted_iota(jnp.int32, (n, size), 0)
    for c in range(pieces):
        result = jnp.zeros((n, size), F32)
        for d in range(ndoc):
            row = c * ndoc + d
            result = jnp.where(replica == rep_ref[d], summed[row:row + 1, :], result)
        next_ref[:, c * size:(c + 1) * size] = result.astype(BF16)
    for copy in sends:
        copy.wait_send()

    def drain(s, carry):
        for piece in range(2):
            @pl.when(line - s >= 0)
            def _():
                owner = 2 * (line - s) + side

                @pl.when(line < half - 1)
                def _():
                    move(0, owner, piece).wait_send()

                move(2, owner, piece).wait_send()

            @pl.when(line + s < half)
            def _():
                owner = 2 * (line + s) + side

                @pl.when(line > 0)
                def _():
                    move(1, owner, piece).wait_send()

                @pl.when(s > 0)
                def _():
                    move(2, owner, piece).wait_send()
        return carry

    lax.fori_loop(0, half, drain, 0)


def local(queries, keys, values, doc_ids, replica_of, step_query, step_key, step_value, out_weight):
    n = lax.axis_size("ctx")
    ntp = lax.axis_size("tp")
    rows, depth = queries.shape
    heads = depth // HD
    kv_dev = max(1, heads // PER)
    tokens = n * rows
    slots = 5 * tokens // 8
    out_columns = out_weight.shape[1]
    width = kv_dev * HD
    pieces = 4 if out_columns % 512 == 0 else 1
    size = out_columns // pieces
    vmem = pl.BlockSpec(memory_space=pltpu.VMEM)
    smem = pl.BlockSpec(memory_space=pltpu.SMEM)
    hbm = pl.BlockSpec(memory_space=pl.ANY)
    share = keys.shape[1] // ntp
    return pl.pallas_call(
        functools.partial(kernel, n, ntp, heads, kv_dev),
        out_shape=(
            jax.ShapeDtypeStruct((rows, depth), BF16),
            jax.ShapeDtypeStruct((n, out_columns), BF16),
            jax.ShapeDtypeStruct((1, share, slots), BF16),
            jax.ShapeDtypeStruct((1, share, slots), BF16),
        ),
        in_specs=[hbm, hbm, hbm, vmem, smem, vmem, vmem, vmem, hbm],
        out_specs=(vmem, vmem, vmem, vmem),
        scratch_shapes=[
            pltpu.VMEM((n, rows, width), BF16),
            pltpu.VMEM((n, rows, width), BF16),
            pltpu.VMEM((rows, depth), BF16),
            pltpu.VMEM((depth, out_columns), BF16),
            pltpu.VMEM((heads, rows, 2 * HD), F32),
            pltpu.VMEM((heads, rows, HD), F32),
            pltpu.VMEM((rows, 2 * rows), F32),
            pltpu.VMEM((rows, rows), F32),
            pltpu.VMEM((heads, 8, HD), F32),
            pltpu.VMEM((kv_dev, 8, HD), F32),
            pltpu.VMEM((kv_dev, 8, HD), F32),
            pltpu.VMEM((16, depth), F32),
            pltpu.VMEM((16, size), F32),
            pltpu.VMEM((pieces, 8, size), F32),
            pltpu.VMEM((16, size), BF16),
            pltpu.VMEM((ntp, 16, size), BF16),
            pltpu.SemaphoreType.DMA((4,)),
            pltpu.SemaphoreType.DMA((3, n, 2)),
            pltpu.SemaphoreType.DMA((n, 2)),
            pltpu.SemaphoreType.DMA((ntp,)),
            pltpu.SemaphoreType.DMA((ntp,)),
        ],
        compiler_params=pltpu.CompilerParams(
            collective_id=0, has_side_effects=True, vmem_limit_bytes=48 * 1024 * 1024
        ),
    )(queries, keys, values, doc_ids.reshape(1, tokens), replica_of, step_query, step_key, step_value, out_weight)


def solution(mesh):
    placed = (
        P("ctx", "tp"),
        P("ctx", None),
        P("ctx", None),
        P(),
        P(),
        P(None, "tp"),
        P(),
        P(),
        P("tp", "ctx"),
    )
    return jax.shard_map(
        local,
        mesh=mesh,
        in_specs=placed,
        out_specs=(P("ctx", "tp"), P(None, "ctx"), P("ctx", "tp", None), P("ctx", "tp", None)),
        check_vma=False,
    )
```

```python
import functools
import math

import jax
import jax.numpy as jnp
from jax import lax
from jax.experimental import pallas as pl
from jax.experimental.pallas import tpu as pltpu
from jax.sharding import PartitionSpec as P

H = 96
KVH = 8
HD = 128
PER = H // KVH
MESH = pl.DeviceIdType.MESH
EXP_SCALE = math.log2(math.e) / math.sqrt(HD)
F32 = jnp.float32
BF16 = jnp.bfloat16
NT = (((1,), (1,)), ((), ()))
NN = (((1,), (0,)), ((), ()))
TN = (((0,), (0,)), ((), ()))


def dot(a, b, dims):
    return lax.dot_general(a, b, dims, preferred_element_type=F32)


def kernel(
    n, ntp, heads, kv_dev,
    q_hbm, k_hbm, v_hbm, doc_hbm, rep_hbm, sq_hbm, sk_hbm, sv_hbm, w_hbm,
    ctx_ref, next_ref, rk_ref, rv_ref,
    kbuf, vbuf, qbuf, wbuf, acc, tops, bias, dstart, sq_scr, sk_scr, sv_scr, att, pack, cut, out_buf, in_buf,
    doc_ref, rep_ref, sq_ref, sk_ref, sv_ref, local_sem, send_sem, recv_sem, part_send, part_recv,
):
    me = lax.axis_index("ctx")
    tp = lax.axis_index("tp")
    half = n // 2
    line = me // 2
    side = me % 2
    mate = 2 * line + 1 - side
    rows = kbuf.shape[1]
    width = kbuf.shape[2]
    per = heads // kv_dev
    first_kv = tp * heads // PER
    tokens = n * rows
    ndoc = sq_ref.shape[0]

    columns = pl.ds(pl.multiple_of(first_kv * HD, HD), width)
    k_copy = pltpu.make_async_copy(k_hbm.at[:, columns], kbuf.at[me], local_sem.at[0])
    v_copy = pltpu.make_async_copy(v_hbm.at[:, columns], vbuf.at[me], local_sem.at[1])
    q_copy = pltpu.make_async_copy(q_hbm, qbuf, local_sem.at[2])
    w_copy = pltpu.make_async_copy(w_hbm, wbuf, local_sem.at[3])
    k_copy.start()
    v_copy.start()
    small = [
        pltpu.make_async_copy(src, dst, local_sem.at[4 + i])
        for i, (src, dst) in enumerate((
            (doc_hbm, doc_ref), (rep_hbm, rep_ref), (sq_hbm, sq_ref), (sk_hbm, sk_ref), (sv_hbm, sv_ref),
        ))
    ]
    for copy in small:
        copy.start()
    q_copy.start()
    w_copy.start()

    barrier = pltpu.get_barrier_semaphore()
    pl.semaphore_signal(barrier, inc=1, device_id={"ctx": mate}, device_id_type=MESH)
    for t in range(1, ntp):
        pl.semaphore_signal(barrier, inc=1, device_id={"tp": lax.rem(tp + t, ntp)}, device_id_type=MESH)

    @pl.when(line > 0)
    def _():
        pl.semaphore_signal(barrier, inc=1, device_id={"ctx": me - 2}, device_id_type=MESH)

    @pl.when(line < half - 1)
    def _():
        pl.semaphore_signal(barrier, inc=1, device_id={"ctx": me + 2}, device_id_type=MESH)

    for copy in small:
        copy.wait()
    docs = doc_ref[...].astype(F32)
    starts = [jnp.sum(jnp.where(docs < d, 1.0, 0.0), axis=1, keepdims=True) for d in range(ndoc + 1)]
    own_docs = doc_ref[:, pl.ds(pl.multiple_of(me * rows, rows), rows)].astype(F32)
    begin = jnp.zeros_like(own_docs)
    for d in range(1, ndoc):
        begin = jnp.where(own_docs == d, starts[d], begin)
    dstart[...] = jnp.transpose(jnp.broadcast_to(begin, (rows, rows)))
    sq_scr[...] = jnp.zeros_like(sq_scr)
    sk_scr[...] = jnp.zeros_like(sk_scr)
    sv_scr[...] = jnp.zeros_like(sv_scr)
    sq = sq_ref[...].astype(F32)
    for h in range(heads):
        sq_scr[h, 0:ndoc, :] = sq[:, h * HD:(h + 1) * HD]
    for g in range(kv_dev):
        head_columns = pl.ds(pl.multiple_of((first_kv + g) * HD, HD), HD)
        sk_scr[g, 0:ndoc, :] = sk_ref[:, head_columns].astype(F32)
        sv_scr[g, 0:ndoc, :] = sv_ref[:, head_columns].astype(F32)
    tops[...] = jnp.full(tops.shape, -1e30, F32)
    acc[...] = jnp.zeros(acc.shape, F32)

    k_copy.wait()
    v_copy.wait()
    q_copy.wait()
    neighbours = 1 + (ntp - 1) + jnp.where(line > 0, 1, 0) + jnp.where(line < half - 1, 1, 0)
    pl.semaphore_wait(barrier, neighbours)

    def move(way, owner, piece):
        buf = (kbuf, vbuf)[piece]
        target = (me + 2, me - 2, mate)[way]
        return pltpu.make_async_remote_copy(
            src_ref=buf.at[owner],
            dst_ref=buf.at[owner],
            send_sem=send_sem.at[way, owner, piece],
            recv_sem=recv_sem.at[owner, piece],
            device_id={"ctx": target},
            device_id_type=MESH,
        )

    for piece in range(2):
        @pl.when(line < half - 1)
        def _():
            move(0, me, piece).start()

        @pl.when(line > 0)
        def _():
            move(1, me, piece).start()

        move(2, me, piece).start()

    def group(o):
        j = 2 * o * rows + lax.broadcasted_iota(jnp.int32, (rows, 2 * rows), 1)
        i = me * rows + lax.broadcasted_iota(jnp.int32, (rows, 2 * rows), 0)
        seen = (j <= i) & (j.astype(F32) >= jnp.concatenate([dstart[...]] * 2, axis=1))
        bias[...] = jnp.where(seen, 0.0, -1e30)
        for g in range(kv_dev):
            lanes = slice(g * HD, (g + 1) * HD)
            k = kbuf[pl.ds(2 * o, 2), :, lanes].reshape(2 * rows, HD)
            v = vbuf[pl.ds(2 * o, 2), :, lanes].reshape(2 * rows, HD)
            v = jnp.concatenate([v, jnp.ones_like(v)], axis=1)

            q = jnp.concatenate(
                [qbuf[:, (g * per + u) * HD:(g * per + u + 1) * HD] for u in range(per)], axis=0
            )
            s = dot(q, k, NT).reshape(per, rows, 2 * rows) + bias[...][None]
            old = tops[g * per:(g + 1) * per]
            top = jnp.maximum(old, jnp.max(s, axis=2, keepdims=True))
            weights = jnp.exp2((s - jnp.concatenate([top, top], axis=2)) * EXP_SCALE)
            fade = jnp.exp2((old - top) * EXP_SCALE)
            tops[g * per:(g + 1) * per] = top
            new = dot(weights.reshape(per * rows, 2 * rows).astype(BF16), v, NN)
            acc[g * per:(g + 1) * per] = (
                acc[g * per:(g + 1) * per] * jnp.concatenate([fade, fade], axis=2)
                + new.reshape(per, rows, 2 * HD)
            )

    back = 5 * n // 8

    def step(s, carry):
        low = line - s
        high = line + s
        for piece in range(2):
            @pl.when(low >= 0)
            def _():
                owner = 2 * low + side
                move(0, owner, piece).wait_recv()

                @pl.when(line < half - 1)
                def _():
                    move(0, owner, piece).start()

                move(2, owner, piece).start()

            @pl.when(high < half)
            def _():
                owner = 2 * high + side
                move(1, owner, piece).wait_recv()

                @pl.when(line > 0)
                def _():
                    move(1, owner, piece).start()

                move(2, owner, piece).start()
        low = line - (s - 1)
        high = line + (s - 1)

        @pl.when(low >= 0)
        def _():
            for piece in range(2):
                move(2, 2 * low + 1 - side, piece).wait_recv()

        @pl.when((high < half) & (s > 1))
        def _():
            for piece in range(2):
                move(2, 2 * high + 1 - side, piece).wait_recv()

        @pl.when((low >= 0) & (2 * low + 1 >= me - back))
        def _():
            group(low)

        return carry

    lax.fori_loop(1, half + 1, step, 0)

    shape = (per * 8, tokens)
    row_doc = (lax.broadcasted_iota(jnp.int32, shape, 0) % 8).astype(F32)
    inside = row_doc == docs
    for g in range(kv_dev):
        lanes = slice(g * HD, (g + 1) * HD)
        k = kbuf[:, :, lanes].reshape(tokens, HD)
        v = vbuf[:, :, lanes].reshape(tokens, HD)
        q = sq_scr[g * per:(g + 1) * per]
        own = jnp.sum(q * sk_scr[g][None], axis=2, keepdims=True).reshape(per * 8, 1)
        s = dot(q.reshape(per * 8, HD).astype(BF16), k, NT)
        top = jnp.maximum(jnp.max(jnp.where(inside, s, -1e30), axis=1, keepdims=True), own)
        weights = jnp.where(inside, jnp.exp2((s - top) * EXP_SCALE), 0.0)
        own_weight = jnp.exp2((own - top) * EXP_SCALE)
        total = jnp.sum(weights, axis=1, keepdims=True) + own_weight
        own_value = jnp.broadcast_to(sv_scr[g][None], (per, 8, HD)).reshape(per * 8, HD)
        mixed = dot(weights.astype(BF16), v, NN) + own_weight.astype(BF16).astype(F32) * own_value
        mixed = mixed / total
        for u in range(per):
            h = g * per + u
            att[0:8, h * HD:(h + 1) * HD] = mixed[u * 8:(u + 1) * 8]
    att[8:16, :] = jnp.zeros((8, heads * HD), F32)

    w_copy.wait()
    pieces = cut.shape[0]
    size = cut.shape[2]
    rows_in = att[...].astype(BF16)
    for c in range(pieces):
        cut[c] = dot(rows_in, wbuf[:, c * size:(c + 1) * size], NN)[0:8]
    pack[...] = jnp.zeros_like(pack)
    for c in range(pieces):
        pack[c * ndoc:(c + 1) * ndoc, :] = cut[c, 0:ndoc, :]
    out_buf[...] = pack[...].astype(BF16)
    sends = []
    for t in range(1, ntp):
        sends.append(pltpu.make_async_remote_copy(
            src_ref=out_buf,
            dst_ref=in_buf.at[t],
            send_sem=part_send.at[t],
            recv_sem=part_recv.at[t],
            device_id={"tp": lax.rem(tp + t, ntp)},
            device_id_type=MESH,
        ))
    for copy in sends:
        copy.start()

    for h in range(heads):
        ctx_ref[:, h * HD:(h + 1) * HD] = (acc[h, :, 0:HD] / acc[h, :, HD:2 * HD]).astype(BF16)

    start = jnp.zeros((1, 1), F32)
    length = jnp.zeros((1, 1), F32)
    for d in range(ndoc):
        named = rep_ref[d] == me
        start = jnp.where(named, starts[d], start)
        length = jnp.where(named, starts[d + 1] - starts[d], length)
    slots = rk_ref.shape[2]
    out_rows = rk_ref.shape[1]
    chunk = slots // max(1, tokens // 1024)
    for first in range(0, slots, chunk):
        slot = (first + lax.broadcasted_iota(jnp.int32, (1, chunk), 1)).astype(F32)
        source = jnp.where(slot < length, slot + start, -1.0)
        position = lax.broadcasted_iota(jnp.int32, (tokens, chunk), 0).astype(F32)
        pick = jnp.where(position == source, 1.0, 0.0).astype(BF16)
        for buf, ref in ((kbuf, rk_ref), (vbuf, rv_ref)):
            taken = dot(buf[...].reshape(tokens, width), pick, TN).astype(BF16)
            if out_rows < width:
                taken = jnp.where(tp % (width // out_rows) == 0, taken[0:out_rows], taken[out_rows:2 * out_rows])
            ref[0, :, first:first + chunk] = taken

    summed = out_buf[...].astype(F32)
    for t in range(1, ntp):
        sends[t - 1].wait_recv()
        summed = summed + in_buf[t].astype(F32)
    replica = lax.broadcasted_iota(jnp.int32, (n, size), 0)
    for c in range(pieces):
        result = jnp.zeros((n, size), F32)
        for d in range(ndoc):
            row = c * ndoc + d
            result = jnp.where(replica == rep_ref[d], summed[row:row + 1, :], result)
        next_ref[:, c * size:(c + 1) * size] = result.astype(BF16)
    for copy in sends:
        copy.wait_send()

    def drain(s, carry):
        for piece in range(2):
            @pl.when(line - s >= 0)
            def _():
                owner = 2 * (line - s) + side

                @pl.when(line < half - 1)
                def _():
                    move(0, owner, piece).wait_send()

                move(2, owner, piece).wait_send()

            @pl.when(line + s < half)
            def _():
                owner = 2 * (line + s) + side

                @pl.when(line > 0)
                def _():
                    move(1, owner, piece).wait_send()

                @pl.when(s > 0)
                def _():
                    move(2, owner, piece).wait_send()
        return carry

    lax.fori_loop(0, half, drain, 0)


def local(queries, keys, values, doc_ids, replica_of, step_query, step_key, step_value, out_weight):
    n = lax.axis_size("ctx")
    ntp = lax.axis_size("tp")
    rows, depth = queries.shape
    heads = depth // HD
    kv_dev = max(1, heads // PER)
    tokens = n * rows
    slots = 5 * tokens // 8
    out_columns = out_weight.shape[1]
    width = kv_dev * HD
    pieces = 4 if out_columns % 512 == 0 else 1
    size = out_columns // pieces
    vmem = pl.BlockSpec(memory_space=pltpu.VMEM)
    hbm = pl.BlockSpec(memory_space=pl.ANY)
    share = keys.shape[1] // ntp
    return pl.pallas_call(
        functools.partial(kernel, n, ntp, heads, kv_dev),
        out_shape=(
            jax.ShapeDtypeStruct((rows, depth), BF16),
            jax.ShapeDtypeStruct((n, out_columns), BF16),
            jax.ShapeDtypeStruct((1, share, slots), BF16),
            jax.ShapeDtypeStruct((1, share, slots), BF16),
        ),
        in_specs=[hbm] * 9,
        out_specs=(vmem, vmem, vmem, vmem),
        scratch_shapes=[
            pltpu.VMEM((n, rows, width), BF16),
            pltpu.VMEM((n, rows, width), BF16),
            pltpu.VMEM((rows, depth), BF16),
            pltpu.VMEM((depth, out_columns), BF16),
            pltpu.VMEM((heads, rows, 2 * HD), F32),
            pltpu.VMEM((heads, rows, HD), F32),
            pltpu.VMEM((rows, 2 * rows), F32),
            pltpu.VMEM((rows, rows), F32),
            pltpu.VMEM((heads, 8, HD), F32),
            pltpu.VMEM((kv_dev, 8, HD), F32),
            pltpu.VMEM((kv_dev, 8, HD), F32),
            pltpu.VMEM((16, depth), F32),
            pltpu.VMEM((16, size), F32),
            pltpu.VMEM((pieces, 8, size), F32),
            pltpu.VMEM((16, size), BF16),
            pltpu.VMEM((ntp, 16, size), BF16),
            pltpu.VMEM((1, tokens), jnp.int32),
            pltpu.SMEM(replica_of.shape, jnp.int32),
            pltpu.VMEM(step_query.shape, BF16),
            pltpu.VMEM(step_key.shape, BF16),
            pltpu.VMEM(step_value.shape, BF16),
            pltpu.SemaphoreType.DMA((9,)),
            pltpu.SemaphoreType.DMA((3, n, 2)),
            pltpu.SemaphoreType.DMA((n, 2)),
            pltpu.SemaphoreType.DMA((ntp,)),
            pltpu.SemaphoreType.DMA((ntp,)),
        ],
        compiler_params=pltpu.CompilerParams(
            collective_id=0, has_side_effects=True, vmem_limit_bytes=60 * 1024 * 1024
        ),
    )(queries, keys, values, doc_ids.reshape(1, tokens), replica_of, step_query, step_key, step_value, out_weight)


def solution(mesh):
    placed = (
        P("ctx", "tp"),
        P("ctx", None),
        P("ctx", None),
        P(),
        P(),
        P(None, "tp"),
        P(),
        P(),
        P("tp", "ctx"),
    )
    return jax.shard_map(
        local,
        mesh=mesh,
        in_specs=placed,
        out_specs=(P("ctx", "tp"), P(None, "ctx"), P("ctx", "tp", None), P("ctx", "tp", None)),
        check_vma=False,
    )
```

```python
import functools
import math

import jax
import jax.numpy as jnp
from jax import lax
from jax.experimental import pallas as pl
from jax.experimental.pallas import tpu as pltpu
from jax.sharding import PartitionSpec as P

H = 96
KVH = 8
HD = 128
PER = H // KVH
MESH = pl.DeviceIdType.MESH
EXP_SCALE = math.log2(math.e) / math.sqrt(HD)
F32 = jnp.float32
BF16 = jnp.bfloat16
NT = (((1,), (1,)), ((), ()))
NN = (((1,), (0,)), ((), ()))
TN = (((0,), (0,)), ((), ()))


def dot(a, b, dims):
    return lax.dot_general(a, b, dims, preferred_element_type=F32)


def kernel(
    n, ntp, heads, kv_dev, combiners,
    q_hbm, k_hbm, v_hbm, doc_hbm, rep_hbm, sq_hbm, sk_hbm, sv_hbm, w_hbm,
    ctx_hbm, next_hbm, rk_hbm, rv_hbm,
    kbuf, vbuf, qbuf, wbuf, acc, tops, bias, dstart, sq_scr, sk_scr, sv_scr, att, pack, cut, out_buf, in_buf,
    part, comb, mixed, ctx_ref, next_ref, rk_ref, rv_ref, out_sem,
    doc_ref, rep_ref, sq_ref, sk_ref, sv_ref, local_sem, send_sem, recv_sem, part_send, part_recv, comb_send, comb_recv, mix_send, mix_recv,
):
    me = lax.axis_index("ctx")
    tp = lax.axis_index("tp")
    half = n // 2
    line = me // 2
    side = me % 2
    mate = 2 * line + 1 - side
    rows = kbuf.shape[1]
    width = kbuf.shape[2]
    per = heads // kv_dev
    first_kv = tp * heads // PER
    tokens = n * rows
    pieces = cut.shape[0]
    size = cut.shape[2]
    ndoc = sq_ref.shape[0]

    columns = pl.ds(pl.multiple_of(first_kv * HD, HD), width)
    k_copy = pltpu.make_async_copy(k_hbm.at[:, columns], kbuf.at[me], local_sem.at[0])
    v_copy = pltpu.make_async_copy(v_hbm.at[:, columns], vbuf.at[me], local_sem.at[1])
    q_copy = pltpu.make_async_copy(q_hbm, qbuf, local_sem.at[2])
    w_copy = pltpu.make_async_copy(w_hbm, wbuf, local_sem.at[3])
    k_copy.start()
    v_copy.start()
    small = [
        pltpu.make_async_copy(src, dst, local_sem.at[4 + i])
        for i, (src, dst) in enumerate((
            (doc_hbm, doc_ref), (rep_hbm, rep_ref), (sq_hbm, sq_ref), (sk_hbm, sk_ref), (sv_hbm, sv_ref),
        ))
    ]
    for copy in small:
        copy.start()
    q_copy.start()
    w_copy.start()

    barrier = pltpu.get_barrier_semaphore()
    for t in range(1, n):
        pl.semaphore_signal(barrier, inc=1, device_id={"ctx": lax.rem(me + t, n)}, device_id_type=MESH)
    for t in range(1, ntp):
        pl.semaphore_signal(barrier, inc=1, device_id={"tp": lax.rem(tp + t, ntp)}, device_id_type=MESH)

    for copy in small:
        copy.wait()
    docs = doc_ref[...].astype(F32)
    starts = [jnp.sum(jnp.where(docs < d, 1.0, 0.0), axis=1, keepdims=True) for d in range(ndoc + 1)]
    own_docs = doc_ref[:, pl.ds(pl.multiple_of(me * rows, rows), rows)].astype(F32)
    begin = jnp.zeros_like(own_docs)
    for d in range(1, ndoc):
        begin = jnp.where(own_docs == d, starts[d], begin)
    dstart[...] = jnp.transpose(jnp.broadcast_to(begin, (rows, rows)))
    sq_scr[...] = jnp.zeros_like(sq_scr)
    sk_scr[...] = jnp.zeros_like(sk_scr)
    sv_scr[...] = jnp.zeros_like(sv_scr)
    sq = sq_ref[...].astype(F32)
    for h in range(heads):
        low = h % 2 * ndoc
        sq_scr[h // 2, low:low + ndoc, :] = sq[:, h * HD:(h + 1) * HD]
    for g in range(kv_dev):
        head_columns = pl.ds(pl.multiple_of((first_kv + g) * HD, HD), HD)
        for low in (0, ndoc):
            sk_scr[g, low:low + ndoc, :] = sk_ref[:, head_columns].astype(F32)
            sv_scr[g, low:low + ndoc, :] = sv_ref[:, head_columns].astype(F32)
    att[...] = jnp.zeros(att.shape, F32)
    tops[...] = jnp.full(tops.shape, -1e30, F32)
    acc[...] = jnp.zeros(acc.shape, F32)

    k_copy.wait()
    v_copy.wait()
    q_copy.wait()
    pl.semaphore_wait(barrier, (n - 1) + (ntp - 1))

    def move(way, owner, piece):
        buf = (kbuf, vbuf)[piece]
        target = (me + 2, me - 2, mate)[way]
        return pltpu.make_async_remote_copy(
            src_ref=buf.at[owner],
            dst_ref=buf.at[owner],
            send_sem=send_sem.at[way, owner, piece],
            recv_sem=recv_sem.at[owner, piece],
            device_id={"ctx": target},
            device_id_type=MESH,
        )

    for piece in range(2):
        @pl.when(line < half - 1)
        def _():
            move(0, me, piece).start()

        @pl.when(line > 0)
        def _():
            move(1, me, piece).start()

        move(2, me, piece).start()

    pairs = heads // 2
    group_pairs = pairs // kv_dev
    share = pairs // combiners
    shape = (group_pairs * 8, rows)
    row_doc = (lax.broadcasted_iota(jnp.int32, shape, 0) % ndoc).astype(F32)
    inside = row_doc == own_docs
    for g in range(kv_dev):
        lanes = slice(g * HD, (g + 1) * HD)
        q = sq_scr[g * group_pairs:(g + 1) * group_pairs].reshape(group_pairs * 8, HD).astype(BF16)
        s = dot(q, kbuf[me, :, lanes], NT)
        top = jnp.max(jnp.where(inside, s, -1e30), axis=1, keepdims=True)
        weights = jnp.where(inside, jnp.exp2((s - top) * EXP_SCALE), 0.0)
        total = jnp.sum(weights, axis=1, keepdims=True)
        summed = dot(weights.astype(BF16), vbuf[me, :, lanes], NN)
        half_lane = lax.broadcasted_iota(jnp.int32, (group_pairs * 8, HD), 1) < HD // 2
        both = jnp.concatenate([summed, jnp.where(half_lane, top, total)], axis=1)
        part[g * group_pairs:(g + 1) * group_pairs] = both.reshape(group_pairs, 8, 2 * HD)

    def to_combiner(t):
        target = lax.rem(me + t, n)
        return pltpu.make_async_remote_copy(
            src_ref=part.at[pl.ds(jnp.minimum(target, combiners - 1) * share, share)],
            dst_ref=comb.at[me],
            send_sem=comb_send.at[t],
            recv_sem=comb_recv.at[me],
            device_id={"ctx": target},
            device_id_type=MESH,
        )

    def from_device(sender):
        return pltpu.make_async_remote_copy(
            src_ref=comb.at[sender],
            dst_ref=comb.at[sender],
            send_sem=comb_send.at[0],
            recv_sem=comb_recv.at[sender],
            device_id={"ctx": mate},
            device_id_type=MESH,
        )

    def mix_copy(t, slot):
        return pltpu.make_async_remote_copy(
            src_ref=mixed.at[slot],
            dst_ref=mixed.at[slot],
            send_sem=mix_send.at[t],
            recv_sem=mix_recv.at[slot],
            device_id={"ctx": lax.rem(me + t, n)},
            device_id_type=MESH,
        )

    for t in range(1, n):
        @pl.when(lax.rem(me + t, n) < combiners)
        def _():
            to_combiner(t).start()

    def combine():
        comb[me] = part[pl.ds(me * share, share)]
        for t in range(1, n):
            from_device(lax.rem(me + t, n)).wait_recv()
        for j in range(share):
            pair = me * share + j
            g = pair // group_pairs
            own = jnp.sum(sq_scr[pair] * sk_scr[g], axis=1, keepdims=True)
            top = own
            for i in range(n):
                top = jnp.maximum(top, comb[i, j, :, HD:HD + 1])
            own_weight = jnp.exp2((own - top) * EXP_SCALE)
            total = own_weight
            summed = own_weight.astype(BF16).astype(F32) * sv_scr[g]
            for i in range(n):
                fade = jnp.exp2((comb[i, j, :, HD:HD + 1] - top) * EXP_SCALE)
                total = total + fade * comb[i, j, :, HD + HD // 2:HD + HD // 2 + 1]
                summed = summed + fade * comb[i, j, :, 0:HD]
            mixed[me, j] = summed / total
        for t in range(1, n):
            mix_copy(t, me).start()

    def project():
        for c in range(combiners):
            @pl.when(c != me)
            def _():
                mix_copy(1, c).wait_recv()
        for h in range(heads):
            low = h % 2 * ndoc
            pair = h // 2
            att[0:ndoc, h * HD:(h + 1) * HD] = mixed[pair // share, pair % share, low:low + ndoc, :]
        w_copy.wait()
        rows_in = att[...].astype(BF16)
        for c in range(pieces):
            cut[c] = dot(rows_in, wbuf[:, c * size:(c + 1) * size], NN)[0:8]
        pack[...] = jnp.zeros_like(pack)
        for c in range(pieces):
            pack[c * ndoc:(c + 1) * ndoc, :] = cut[c, 0:ndoc, :]
        out_buf[...] = pack[...].astype(BF16)
        for t in range(1, ntp):
            term(t).start()

    def term(t):
        return pltpu.make_async_remote_copy(
            src_ref=out_buf,
            dst_ref=in_buf.at[t],
            send_sem=part_send.at[t],
            recv_sem=part_recv.at[t],
            device_id={"tp": lax.rem(tp + t, ntp)},
            device_id_type=MESH,
        )

    def group(o):
        j = 2 * o * rows + lax.broadcasted_iota(jnp.int32, (rows, 2 * rows), 1)
        i = me * rows + lax.broadcasted_iota(jnp.int32, (rows, 2 * rows), 0)
        seen = (j <= i) & (j.astype(F32) >= jnp.concatenate([dstart[...]] * 2, axis=1))
        bias[...] = jnp.where(seen, 0.0, -1e30)
        for g in range(kv_dev):
            lanes = slice(g * HD, (g + 1) * HD)
            k = kbuf[pl.ds(2 * o, 2), :, lanes].reshape(2 * rows, HD)
            v = vbuf[pl.ds(2 * o, 2), :, lanes].reshape(2 * rows, HD)
            v = jnp.concatenate([v, jnp.ones_like(v)], axis=1)

            q = jnp.concatenate(
                [qbuf[:, (g * per + u) * HD:(g * per + u + 1) * HD] for u in range(per)], axis=0
            )
            s = dot(q, k, NT).reshape(per, rows, 2 * rows) + bias[...][None]
            old = tops[g * per:(g + 1) * per]
            top = jnp.maximum(old, jnp.max(s, axis=2, keepdims=True))
            weights = jnp.exp2((s - jnp.concatenate([top, top], axis=2)) * EXP_SCALE)
            fade = jnp.exp2((old - top) * EXP_SCALE)
            tops[g * per:(g + 1) * per] = top
            new = dot(weights.reshape(per * rows, 2 * rows).astype(BF16), v, NN)
            acc[g * per:(g + 1) * per] = (
                acc[g * per:(g + 1) * per] * jnp.concatenate([fade, fade], axis=2)
                + new.reshape(per, rows, 2 * HD)
            )

    back = 5 * n // 8

    def step(s, carry):
        low = line - s
        high = line + s
        for piece in range(2):
            @pl.when(low >= 0)
            def _():
                owner = 2 * low + side
                move(0, owner, piece).wait_recv()

                @pl.when(line < half - 1)
                def _():
                    move(0, owner, piece).start()

                move(2, owner, piece).start()

            @pl.when(high < half)
            def _():
                owner = 2 * high + side
                move(1, owner, piece).wait_recv()

                @pl.when(line > 0)
                def _():
                    move(1, owner, piece).start()

                move(2, owner, piece).start()
        @pl.when(s == half - 1)
        def _():
            project()

        low = line - (s - 1)
        high = line + (s - 1)

        @pl.when(low >= 0)
        def _():
            for piece in range(2):
                move(2, 2 * low + 1 - side, piece).wait_recv()

        @pl.when((high < half) & (s > 1))
        def _():
            for piece in range(2):
                move(2, 2 * high + 1 - side, piece).wait_recv()

        @pl.when((low >= 0) & (2 * low + 1 >= me - back))
        def _():
            group(low)

        @pl.when((s == 1) & (me < combiners))
        def _():
            combine()

        return carry

    lax.fori_loop(1, half + 1, step, 0)

    for h in range(heads):
        ctx_ref[:, h * HD:(h + 1) * HD] = (acc[h, :, 0:HD] / acc[h, :, HD:2 * HD]).astype(BF16)

    results = [
        pltpu.make_async_copy(src, dst, out_sem.at[i])
        for i, (src, dst) in enumerate((
            (ctx_ref, ctx_hbm), (rk_ref, rk_hbm), (rv_ref, rv_hbm), (next_ref, next_hbm),
        ))
    ]
    results[0].start()

    start = jnp.zeros((1, 1), F32)
    length = jnp.zeros((1, 1), F32)
    for d in range(ndoc):
        named = rep_ref[d] == me
        start = jnp.where(named, starts[d], start)
        length = jnp.where(named, starts[d + 1] - starts[d], length)
    slots = rk_ref.shape[2]
    out_rows = rk_ref.shape[1]
    chunk = slots // max(1, tokens // 1024)
    for first in range(0, slots, chunk):
        slot = (first + lax.broadcasted_iota(jnp.int32, (1, chunk), 1)).astype(F32)
        source = jnp.where(slot < length, slot + start, -1.0)
        position = lax.broadcasted_iota(jnp.int32, (tokens, chunk), 0).astype(F32)
        pick = jnp.where(position == source, 1.0, 0.0).astype(BF16)
        for buf, ref in ((kbuf, rk_ref), (vbuf, rv_ref)):
            taken = dot(buf[...].reshape(tokens, width), pick, TN).astype(BF16)
            if out_rows < width:
                taken = jnp.where(tp % (width // out_rows) == 0, taken[0:out_rows], taken[out_rows:2 * out_rows])
            ref[0, :, first:first + chunk] = taken

    results[1].start()
    results[2].start()

    summed = out_buf[...].astype(F32)
    for t in range(1, ntp):
        term(t).wait_recv()
        summed = summed + in_buf[t].astype(F32)
    replica = lax.broadcasted_iota(jnp.int32, (n, size), 0)
    for c in range(pieces):
        result = jnp.zeros((n, size), F32)
        for d in range(ndoc):
            row = c * ndoc + d
            result = jnp.where(replica == rep_ref[d], summed[row:row + 1, :], result)
        next_ref[:, c * size:(c + 1) * size] = result.astype(BF16)
    results[3].start()
    for t in range(1, ntp):
        term(t).wait_send()
    for t in range(1, n):
        @pl.when(lax.rem(me + t, n) < combiners)
        def _():
            to_combiner(t).wait_send()

        @pl.when(me < combiners)
        def _():
            mix_copy(t, me).wait_send()

    def drain(s, carry):
        for piece in range(2):
            @pl.when(line - s >= 0)
            def _():
                owner = 2 * (line - s) + side

                @pl.when(line < half - 1)
                def _():
                    move(0, owner, piece).wait_send()

                move(2, owner, piece).wait_send()

            @pl.when(line + s < half)
            def _():
                owner = 2 * (line + s) + side

                @pl.when(line > 0)
                def _():
                    move(1, owner, piece).wait_send()

                @pl.when(s > 0)
                def _():
                    move(2, owner, piece).wait_send()
        return carry

    lax.fori_loop(0, half, drain, 0)
    for copy in results:
        copy.wait()


def deliver(*refs):
    copies = [pltpu.make_async_copy(refs[i], refs[4 + i], refs[8].at[i]) for i in range(4)]
    for copy in copies:
        copy.start()
    for copy in copies:
        copy.wait()


def local(queries, keys, values, doc_ids, replica_of, step_query, step_key, step_value, out_weight):
    n = lax.axis_size("ctx")
    ntp = lax.axis_size("tp")
    rows, depth = queries.shape
    heads = depth // HD
    kv_dev = max(1, heads // PER)
    tokens = n * rows
    slots = 5 * tokens // 8
    out_columns = out_weight.shape[1]
    width = kv_dev * HD
    pieces = 4 if out_columns % 512 == 0 else 1
    size = out_columns // pieces
    hbm = pl.BlockSpec(memory_space=pl.ANY)
    share = keys.shape[1] // ntp
    pairs = heads // 2
    combiners = max(c for c in range(1, n + 1) if pairs % c == 0)
    results = pl.pallas_call(
        functools.partial(kernel, n, ntp, heads, kv_dev, combiners),
        out_shape=(
            jax.ShapeDtypeStruct((rows, depth), BF16),
            jax.ShapeDtypeStruct((n, out_columns), BF16),
            jax.ShapeDtypeStruct((1, share, slots), BF16),
            jax.ShapeDtypeStruct((1, share, slots), BF16),
        ),
        in_specs=[hbm] * 9,
        out_specs=(hbm,) * 4,
        scratch_shapes=[
            pltpu.VMEM((n, rows, width), BF16),
            pltpu.VMEM((n, rows, width), BF16),
            pltpu.VMEM((rows, depth), BF16),
            pltpu.VMEM((depth, out_columns), BF16),
            pltpu.VMEM((heads, rows, 2 * HD), F32),
            pltpu.VMEM((heads, rows, HD), F32),
            pltpu.VMEM((rows, 2 * rows), F32),
            pltpu.VMEM((rows, rows), F32),
            pltpu.VMEM((pairs, 8, HD), F32),
            pltpu.VMEM((kv_dev, 8, HD), F32),
            pltpu.VMEM((kv_dev, 8, HD), F32),
            pltpu.VMEM((16, depth), F32),
            pltpu.VMEM((16, size), F32),
            pltpu.VMEM((pieces, 8, size), F32),
            pltpu.VMEM((16, size), BF16),
            pltpu.VMEM((ntp, 16, size), BF16),
            pltpu.VMEM((pairs, 8, 2 * HD), F32),
            pltpu.VMEM((n, pairs // combiners, 8, 2 * HD), F32),
            pltpu.VMEM((combiners, pairs // combiners, 8, HD), F32),
            pltpu.VMEM((rows, depth), BF16),
            pltpu.VMEM((n, out_columns), BF16),
            pltpu.VMEM((1, share, slots), BF16),
            pltpu.VMEM((1, share, slots), BF16),
            pltpu.SemaphoreType.DMA((4,)),
            pltpu.VMEM((1, tokens), jnp.int32),
            pltpu.SMEM(replica_of.shape, jnp.int32),
            pltpu.VMEM(step_query.shape, BF16),
            pltpu.VMEM(step_key.shape, BF16),
            pltpu.VMEM(step_value.shape, BF16),
            pltpu.SemaphoreType.DMA((9,)),
            pltpu.SemaphoreType.DMA((3, n, 2)),
            pltpu.SemaphoreType.DMA((n, 2)),
            pltpu.SemaphoreType.DMA((ntp,)),
            pltpu.SemaphoreType.DMA((ntp,)),
            pltpu.SemaphoreType.DMA((n,)),
            pltpu.SemaphoreType.DMA((n,)),
            pltpu.SemaphoreType.DMA((n,)),
            pltpu.SemaphoreType.DMA((n,)),
        ],
        compiler_params=pltpu.CompilerParams(
            collective_id=0, has_side_effects=True, vmem_limit_bytes=60 * 1024 * 1024
        ),
    )(queries, keys, values, doc_ids.reshape(1, tokens), replica_of, step_query, step_key, step_value, out_weight)
    return pl.pallas_call(
        deliver,
        out_shape=tuple(jax.ShapeDtypeStruct(r.shape, r.dtype) for r in results),
        in_specs=[hbm] * 4,
        out_specs=(hbm,) * 4,
        scratch_shapes=[pltpu.SemaphoreType.DMA((4,))],
        compiler_params=pltpu.CompilerParams(vmem_limit_bytes=60 * 1024 * 1024),
    )(*results)


def solution(mesh):
    placed = (
        P("ctx", "tp"),
        P("ctx", None),
        P("ctx", None),
        P(),
        P(),
        P(None, "tp"),
        P(),
        P(),
        P("tp", "ctx"),
    )
    return jax.shard_map(
        local,
        mesh=mesh,
        in_specs=placed,
        out_specs=(P("ctx", "tp"), P(None, "ctx"), P("ctx", "tp", None), P("ctx", "tp", None)),
        check_vma=False,
    )
```

```python
import functools
import math

import jax
import jax.numpy as jnp
from jax import lax
from jax.experimental import pallas as pl
from jax.experimental.pallas import tpu as pltpu
from jax.sharding import PartitionSpec as P

H = 96
KVH = 8
HD = 128
PER = H // KVH
MESH = pl.DeviceIdType.MESH
EXP_SCALE = math.log2(math.e) / math.sqrt(HD)
F32 = jnp.float32
BF16 = jnp.bfloat16
NT = (((1,), (1,)), ((), ()))
NN = (((1,), (0,)), ((), ()))
TN = (((0,), (0,)), ((), ()))


def dot(a, b, dims):
    return lax.dot_general(a, b, dims, preferred_element_type=F32)


def kernel(
    n, ntp, heads, kv_dev, combiners,
    q_hbm, k_hbm, v_hbm, doc_hbm, rep_hbm, sq_hbm, sk_hbm, sv_hbm, w_hbm,
    ctx_hbm, next_hbm, rk_hbm, rv_hbm,
    kbuf, vbuf, qbuf, wbuf, acc, tops, bias, dstart, sq_scr, sk_scr, sv_scr, att, pack, cut, out_buf, in_buf,
    part, comb, mixed, ctx_ref, next_ref, rk_ref, rv_ref, out_sem,
    doc_ref, rep_ref, sq_ref, sk_ref, sv_ref, local_sem, send_sem, recv_sem, part_send, part_recv, comb_send, comb_recv, mix_send, mix_recv,
):
    me = lax.axis_index("ctx")
    tp = lax.axis_index("tp")
    half = n // 2
    line = me // 2
    side = me % 2
    mate = 2 * line + 1 - side
    rows = kbuf.shape[1]
    width = kbuf.shape[2]
    per = heads // kv_dev
    first_kv = tp * heads // PER
    tokens = n * rows
    pieces = cut.shape[0]
    size = cut.shape[2]
    ndoc = sq_ref.shape[0]

    columns = pl.ds(pl.multiple_of(first_kv * HD, HD), width)
    k_copy = pltpu.make_async_copy(k_hbm.at[:, columns], kbuf.at[me], local_sem.at[0])
    v_copy = pltpu.make_async_copy(v_hbm.at[:, columns], vbuf.at[me], local_sem.at[1])
    q_copy = pltpu.make_async_copy(q_hbm, qbuf, local_sem.at[2])
    w_copy = pltpu.make_async_copy(w_hbm, wbuf, local_sem.at[3])
    k_copy.start()
    v_copy.start()
    small = [
        pltpu.make_async_copy(src, dst, local_sem.at[4 + i])
        for i, (src, dst) in enumerate((
            (doc_hbm, doc_ref), (rep_hbm, rep_ref), (sq_hbm, sq_ref), (sk_hbm, sk_ref), (sv_hbm, sv_ref),
        ))
    ]
    for copy in small:
        copy.start()

    barrier = pltpu.get_barrier_semaphore()
    for t in range(1, n):
        pl.semaphore_signal(barrier, inc=1, device_id={"ctx": lax.rem(me + t, n)}, device_id_type=MESH)
    for t in range(1, ntp):
        pl.semaphore_signal(barrier, inc=1, device_id={"tp": lax.rem(tp + t, ntp)}, device_id_type=MESH)

    pl.semaphore_wait(barrier, (n - 1) + (ntp - 1))

    def move(way, owner, piece):
        buf = (kbuf, vbuf)[piece]
        target = (me + 2, me - 2, mate)[way]
        return pltpu.make_async_remote_copy(
            src_ref=buf.at[owner],
            dst_ref=buf.at[owner],
            send_sem=send_sem.at[way, owner, piece],
            recv_sem=recv_sem.at[owner, piece],
            device_id={"ctx": target},
            device_id_type=MESH,
        )

    def move_own(way, piece):
        target = (me + 2, me - 2, mate)[way]
        return pltpu.make_async_remote_copy(
            src_ref=(k_hbm, v_hbm)[piece].at[:, columns],
            dst_ref=(kbuf, vbuf)[piece].at[me],
            send_sem=send_sem.at[way, me, piece],
            recv_sem=recv_sem.at[me, piece],
            device_id={"ctx": target},
            device_id_type=MESH,
        )

    for piece in range(2):
        @pl.when(line < half - 1)
        def _():
            move_own(0, piece).start()

        @pl.when(line > 0)
        def _():
            move_own(1, piece).start()

        move_own(2, piece).start()
    q_copy.start()
    w_copy.start()

    for copy in small:
        copy.wait()
    docs = doc_ref[...].astype(F32)
    starts = [jnp.sum(jnp.where(docs < d, 1.0, 0.0), axis=1, keepdims=True) for d in range(ndoc + 1)]
    own_docs = doc_ref[:, pl.ds(pl.multiple_of(me * rows, rows), rows)].astype(F32)
    begin = jnp.zeros_like(own_docs)
    for d in range(1, ndoc):
        begin = jnp.where(own_docs == d, starts[d], begin)
    dstart[...] = jnp.transpose(jnp.broadcast_to(begin, (rows, rows)))
    sq_scr[...] = jnp.zeros_like(sq_scr)
    sk_scr[...] = jnp.zeros_like(sk_scr)
    sv_scr[...] = jnp.zeros_like(sv_scr)
    sq = sq_ref[...].astype(F32)
    for h in range(heads):
        low = h % 2 * ndoc
        sq_scr[h // 2, low:low + ndoc, :] = sq[:, h * HD:(h + 1) * HD]
    for g in range(kv_dev):
        head_columns = pl.ds(pl.multiple_of((first_kv + g) * HD, HD), HD)
        for low in (0, ndoc):
            sk_scr[g, low:low + ndoc, :] = sk_ref[:, head_columns].astype(F32)
            sv_scr[g, low:low + ndoc, :] = sv_ref[:, head_columns].astype(F32)
    att[...] = jnp.zeros(att.shape, F32)

    k_copy.wait()
    v_copy.wait()

    pairs = heads // 2
    group_pairs = pairs // kv_dev
    share = pairs // combiners
    shape = (group_pairs * 8, rows)
    row_doc = (lax.broadcasted_iota(jnp.int32, shape, 0) % ndoc).astype(F32)
    inside = row_doc == own_docs
    for g in range(kv_dev):
        lanes = slice(g * HD, (g + 1) * HD)
        q = sq_scr[g * group_pairs:(g + 1) * group_pairs].reshape(group_pairs * 8, HD).astype(BF16)
        s = dot(q, kbuf[me, :, lanes], NT)
        top = jnp.max(jnp.where(inside, s, -1e30), axis=1, keepdims=True)
        weights = jnp.where(inside, jnp.exp2((s - top) * EXP_SCALE), 0.0)
        total = jnp.sum(weights, axis=1, keepdims=True)
        summed = dot(weights.astype(BF16), vbuf[me, :, lanes], NN)
        half_lane = lax.broadcasted_iota(jnp.int32, (group_pairs * 8, HD), 1) < HD // 2
        both = jnp.concatenate([summed, jnp.where(half_lane, top, total)], axis=1)
        part[g * group_pairs:(g + 1) * group_pairs] = both.reshape(group_pairs, 8, 2 * HD)

    def to_combiner(t):
        target = lax.rem(me + t, n)
        return pltpu.make_async_remote_copy(
            src_ref=part.at[pl.ds(jnp.minimum(target, combiners - 1) * share, share)],
            dst_ref=comb.at[me],
            send_sem=comb_send.at[t],
            recv_sem=comb_recv.at[me],
            device_id={"ctx": target},
            device_id_type=MESH,
        )

    def from_device(sender):
        return pltpu.make_async_remote_copy(
            src_ref=comb.at[sender],
            dst_ref=comb.at[sender],
            send_sem=comb_send.at[0],
            recv_sem=comb_recv.at[sender],
            device_id={"ctx": mate},
            device_id_type=MESH,
        )

    def mix_copy(t, slot):
        return pltpu.make_async_remote_copy(
            src_ref=mixed.at[slot],
            dst_ref=mixed.at[slot],
            send_sem=mix_send.at[t],
            recv_sem=mix_recv.at[slot],
            device_id={"ctx": lax.rem(me + t, n)},
            device_id_type=MESH,
        )

    for t in range(1, n):
        @pl.when(lax.rem(me + t, n) < combiners)
        def _():
            to_combiner(t).start()

    tops[...] = jnp.full(tops.shape, -1e30, F32)
    acc[...] = jnp.zeros(acc.shape, F32)

    def combine():
        comb[me] = part[pl.ds(me * share, share)]
        for t in range(1, n):
            from_device(lax.rem(me + t, n)).wait_recv()
        for j in range(share):
            pair = me * share + j
            g = pair // group_pairs
            own = jnp.sum(sq_scr[pair] * sk_scr[g], axis=1, keepdims=True)
            top = own
            for i in range(n):
                top = jnp.maximum(top, comb[i, j, :, HD:HD + 1])
            own_weight = jnp.exp2((own - top) * EXP_SCALE)
            total = own_weight
            summed = own_weight.astype(BF16).astype(F32) * sv_scr[g]
            for i in range(n):
                fade = jnp.exp2((comb[i, j, :, HD:HD + 1] - top) * EXP_SCALE)
                total = total + fade * comb[i, j, :, HD + HD // 2:HD + HD // 2 + 1]
                summed = summed + fade * comb[i, j, :, 0:HD]
            mixed[me, j] = summed / total
        for t in range(1, n):
            mix_copy(t, me).start()

    def project():
        for c in range(combiners):
            @pl.when(c != me)
            def _():
                mix_copy(1, c).wait_recv()
        for h in range(heads):
            low = h % 2 * ndoc
            pair = h // 2
            att[0:ndoc, h * HD:(h + 1) * HD] = mixed[pair // share, pair % share, low:low + ndoc, :]
        w_copy.wait()
        rows_in = att[...].astype(BF16)
        for c in range(pieces):
            cut[c] = dot(rows_in, wbuf[:, c * size:(c + 1) * size], NN)[0:8]
        pack[...] = jnp.zeros_like(pack)
        for c in range(pieces):
            pack[c * ndoc:(c + 1) * ndoc, :] = cut[c, 0:ndoc, :]
        out_buf[...] = pack[...].astype(BF16)
        for t in range(1, ntp):
            term(t).start()

    def term(t):
        return pltpu.make_async_remote_copy(
            src_ref=out_buf,
            dst_ref=in_buf.at[t],
            send_sem=part_send.at[t],
            recv_sem=part_recv.at[t],
            device_id={"tp": lax.rem(tp + t, ntp)},
            device_id_type=MESH,
        )

    def group(o):
        j = 2 * o * rows + lax.broadcasted_iota(jnp.int32, (rows, 2 * rows), 1)
        i = me * rows + lax.broadcasted_iota(jnp.int32, (rows, 2 * rows), 0)
        seen = (j <= i) & (j.astype(F32) >= jnp.concatenate([dstart[...]] * 2, axis=1))
        bias[...] = jnp.where(seen, 0.0, -1e30)
        for g in range(kv_dev):
            lanes = slice(g * HD, (g + 1) * HD)
            k = kbuf[pl.ds(2 * o, 2), :, lanes].reshape(2 * rows, HD)
            v = vbuf[pl.ds(2 * o, 2), :, lanes].reshape(2 * rows, HD)
            v = jnp.concatenate([v, jnp.ones_like(v)], axis=1)

            q = jnp.concatenate(
                [qbuf[:, (g * per + u) * HD:(g * per + u + 1) * HD] for u in range(per)], axis=0
            )
            s = dot(q, k, NT).reshape(per, rows, 2 * rows) + bias[...][None]
            old = tops[g * per:(g + 1) * per]
            top = jnp.maximum(old, jnp.max(s, axis=2, keepdims=True))
            weights = jnp.exp2((s - jnp.concatenate([top, top], axis=2)) * EXP_SCALE)
            fade = jnp.exp2((old - top) * EXP_SCALE)
            tops[g * per:(g + 1) * per] = top
            new = dot(weights.reshape(per * rows, 2 * rows).astype(BF16), v, NN)
            acc[g * per:(g + 1) * per] = (
                acc[g * per:(g + 1) * per] * jnp.concatenate([fade, fade], axis=2)
                + new.reshape(per, rows, 2 * HD)
            )

    results = [
        pltpu.make_async_copy(src, dst, out_sem.at[i])
        for i, (src, dst) in enumerate((
            (ctx_ref, ctx_hbm), (rk_ref, rk_hbm), (rv_ref, rv_hbm), (next_ref, next_hbm),
        ))
    ]
    def finish():
        for h in range(heads):
            ctx_ref[:, h * HD:(h + 1) * HD] = (acc[h, :, 0:HD] / acc[h, :, HD:2 * HD]).astype(BF16)
        results[0].start()

    back = 5 * n // 8
    late = (line >= half - 1) & (2 * (line - half) + 3 >= me - back)

    def step(s, carry):
        low = line - s
        high = line + s
        for piece in range(2):
            @pl.when(low >= 0)
            def _():
                owner = 2 * low + side
                move(0, owner, piece).wait_recv()

                @pl.when(line < half - 1)
                def _():
                    move(0, owner, piece).start()

                move(2, owner, piece).start()

            @pl.when(high < half)
            def _():
                owner = 2 * high + side
                move(1, owner, piece).wait_recv()

                @pl.when(line > 0)
                def _():
                    move(1, owner, piece).start()

                move(2, owner, piece).start()
        @pl.when(s == half - 1)
        def _():
            project()

        @pl.when((s == half) & jnp.logical_not(late))
        def _():
            finish()

        low = line - (s - 1)
        high = line + (s - 1)

        @pl.when(low >= 0)
        def _():
            for piece in range(2):
                move(2, 2 * low + 1 - side, piece).wait_recv()

        @pl.when((high < half) & (s > 1))
        def _():
            for piece in range(2):
                move(2, 2 * high + 1 - side, piece).wait_recv()

        @pl.when((low >= 0) & (2 * low + 1 >= me - back))
        def _():
            group(low)

        @pl.when((s == half) & late)
        def _():
            finish()

        @pl.when((s == 1) & (me < combiners))
        def _():
            combine()

        return carry

    q_copy.wait()
    lax.fori_loop(1, half + 1, step, 0)

    start = jnp.zeros((1, 1), F32)
    length = jnp.zeros((1, 1), F32)
    for d in range(ndoc):
        named = rep_ref[d] == me
        start = jnp.where(named, starts[d], start)
        length = jnp.where(named, starts[d + 1] - starts[d], length)
    slots = rk_ref.shape[2]
    out_rows = rk_ref.shape[1]
    chunk = slots // max(1, tokens // 1024)
    for first in range(0, slots, chunk):
        slot = (first + lax.broadcasted_iota(jnp.int32, (1, chunk), 1)).astype(F32)
        source = jnp.where(slot < length, slot + start, -1.0)
        position = lax.broadcasted_iota(jnp.int32, (tokens, chunk), 0).astype(F32)
        pick = jnp.where(position == source, 1.0, 0.0).astype(BF16)
        for buf, ref in ((kbuf, rk_ref), (vbuf, rv_ref)):
            taken = dot(buf[...].reshape(tokens, width), pick, TN).astype(BF16)
            if out_rows < width:
                taken = jnp.where(tp % (width // out_rows) == 0, taken[0:out_rows], taken[out_rows:2 * out_rows])
            ref[0, :, first:first + chunk] = taken

    results[1].start()
    results[2].start()

    summed = out_buf[...].astype(F32)
    for t in range(1, ntp):
        term(t).wait_recv()
        summed = summed + in_buf[t].astype(F32)
    replica = lax.broadcasted_iota(jnp.int32, (n, size), 0)
    for c in range(pieces):
        result = jnp.zeros((n, size), F32)
        for d in range(ndoc):
            row = c * ndoc + d
            result = jnp.where(replica == rep_ref[d], summed[row:row + 1, :], result)
        next_ref[:, c * size:(c + 1) * size] = result.astype(BF16)
    results[3].start()
    for t in range(1, ntp):
        term(t).wait_send()
    for t in range(1, n):
        @pl.when(lax.rem(me + t, n) < combiners)
        def _():
            to_combiner(t).wait_send()

        @pl.when(me < combiners)
        def _():
            mix_copy(t, me).wait_send()

    def drain(s, carry):
        for piece in range(2):
            @pl.when(line - s >= 0)
            def _():
                owner = 2 * (line - s) + side

                @pl.when(line < half - 1)
                def _():
                    move(0, owner, piece).wait_send()

                move(2, owner, piece).wait_send()

            @pl.when(line + s < half)
            def _():
                owner = 2 * (line + s) + side

                @pl.when(line > 0)
                def _():
                    move(1, owner, piece).wait_send()

                @pl.when(s > 0)
                def _():
                    move(2, owner, piece).wait_send()
        return carry

    lax.fori_loop(0, half, drain, 0)
    for copy in results:
        copy.wait()


def deliver(*refs):
    inward = [pltpu.make_async_copy(refs[i], refs[8 + i], refs[12].at[i]) for i in range(4)]
    outward = [pltpu.make_async_copy(refs[8 + i], refs[4 + i], refs[12].at[4 + i]) for i in range(4)]
    for copy in inward:
        copy.start()
    for i in range(4):
        inward[i].wait()
        outward[i].start()
    for copy in outward:
        copy.wait()


def local(queries, keys, values, doc_ids, replica_of, step_query, step_key, step_value, out_weight):
    n = lax.axis_size("ctx")
    ntp = lax.axis_size("tp")
    rows, depth = queries.shape
    heads = depth // HD
    kv_dev = max(1, heads // PER)
    tokens = n * rows
    slots = 5 * tokens // 8
    out_columns = out_weight.shape[1]
    width = kv_dev * HD
    pieces = 4 if out_columns % 512 == 0 else 1
    size = out_columns // pieces
    hbm = pl.BlockSpec(memory_space=pl.ANY)
    share = keys.shape[1] // ntp
    pairs = heads // 2
    combiners = max(c for c in range(1, n + 1) if pairs % c == 0)
    results = pl.pallas_call(
        functools.partial(kernel, n, ntp, heads, kv_dev, combiners),
        out_shape=(
            jax.ShapeDtypeStruct((rows, depth), BF16),
            jax.ShapeDtypeStruct((n, out_columns), BF16),
            jax.ShapeDtypeStruct((1, share, slots), BF16),
            jax.ShapeDtypeStruct((1, share, slots), BF16),
        ),
        in_specs=[hbm] * 9,
        out_specs=(hbm,) * 4,
        scratch_shapes=[
            pltpu.VMEM((n, rows, width), BF16),
            pltpu.VMEM((n, rows, width), BF16),
            pltpu.VMEM((rows, depth), BF16),
            pltpu.VMEM((depth, out_columns), BF16),
            pltpu.VMEM((heads, rows, 2 * HD), F32),
            pltpu.VMEM((heads, rows, HD), F32),
            pltpu.VMEM((rows, 2 * rows), F32),
            pltpu.VMEM((rows, rows), F32),
            pltpu.VMEM((pairs, 8, HD), F32),
            pltpu.VMEM((kv_dev, 8, HD), F32),
            pltpu.VMEM((kv_dev, 8, HD), F32),
            pltpu.VMEM((16, depth), F32),
            pltpu.VMEM((16, size), F32),
            pltpu.VMEM((pieces, 8, size), F32),
            pltpu.VMEM((16, size), BF16),
            pltpu.VMEM((ntp, 16, size), BF16),
            pltpu.VMEM((pairs, 8, 2 * HD), F32),
            pltpu.VMEM((n, pairs // combiners, 8, 2 * HD), F32),
            pltpu.VMEM((combiners, pairs // combiners, 8, HD), F32),
            pltpu.VMEM((rows, depth), BF16),
            pltpu.VMEM((n, out_columns), BF16),
            pltpu.VMEM((1, share, slots), BF16),
            pltpu.VMEM((1, share, slots), BF16),
            pltpu.SemaphoreType.DMA((4,)),
            pltpu.VMEM((1, tokens), jnp.int32),
            pltpu.SMEM(replica_of.shape, jnp.int32),
            pltpu.VMEM(step_query.shape, BF16),
            pltpu.VMEM(step_key.shape, BF16),
            pltpu.VMEM(step_value.shape, BF16),
            pltpu.SemaphoreType.DMA((9,)),
            pltpu.SemaphoreType.DMA((3, n, 2)),
            pltpu.SemaphoreType.DMA((n, 2)),
            pltpu.SemaphoreType.DMA((ntp,)),
            pltpu.SemaphoreType.DMA((ntp,)),
            pltpu.SemaphoreType.DMA((n,)),
            pltpu.SemaphoreType.DMA((n,)),
            pltpu.SemaphoreType.DMA((n,)),
            pltpu.SemaphoreType.DMA((n,)),
        ],
        compiler_params=pltpu.CompilerParams(
            collective_id=0, has_side_effects=True, vmem_limit_bytes=60 * 1024 * 1024
        ),
    )(queries, keys, values, doc_ids.reshape(1, tokens), replica_of, step_query, step_key, step_value, out_weight)
    return pl.pallas_call(
        deliver,
        out_shape=tuple(jax.ShapeDtypeStruct(r.shape, r.dtype) for r in results),
        in_specs=[hbm] * 4,
        out_specs=(hbm,) * 4,
        scratch_shapes=[pltpu.VMEM(r.shape, r.dtype) for r in results] + [pltpu.SemaphoreType.DMA((8,))],
        compiler_params=pltpu.CompilerParams(vmem_limit_bytes=60 * 1024 * 1024),
    )(*results)


def solution(mesh):
    placed = (
        P("ctx", "tp"),
        P("ctx", None),
        P("ctx", None),
        P(),
        P(),
        P(None, "tp"),
        P(),
        P(),
        P("tp", "ctx"),
    )
    return jax.shard_map(
        local,
        mesh=mesh,
        in_specs=placed,
        out_specs=(P("ctx", "tp"), P(None, "ctx"), P("ctx", "tp", None), P("ctx", "tp", None)),
        check_vma=False,
    )
```

```python
import functools
import math

import jax
import jax.numpy as jnp
from jax import lax
from jax.experimental import pallas as pl
from jax.experimental.pallas import tpu as pltpu
from jax.sharding import PartitionSpec as P

H = 96
KVH = 8
HD = 128
PER = H // KVH
MESH = pl.DeviceIdType.MESH
EXP_SCALE = math.log2(math.e) / math.sqrt(HD)
F32 = jnp.float32
BF16 = jnp.bfloat16
NT = (((1,), (1,)), ((), ()))
NN = (((1,), (0,)), ((), ()))
TN = (((0,), (0,)), ((), ()))


def dot(a, b, dims):
    return lax.dot_general(a, b, dims, preferred_element_type=F32)


def kernel(
    n, ntp, heads, kv_dev, combiners,
    q_hbm, k_hbm, v_hbm, doc_hbm, rep_hbm, sq_hbm, sk_hbm, sv_hbm, w_hbm,
    ctx_hbm, next_hbm, rk_hbm, rv_hbm,
    kbuf, vbuf, qbuf, wbuf, acc, tops, bias, dstart, sq_scr, sk_scr, sv_scr, att, pack, cut, out_buf, in_buf,
    part, comb, mixed, pick, kt, vt, ctx_ref, next_ref, rk_ref, rv_ref, out_sem,
    doc_ref, rep_ref, sq_ref, sk_ref, sv_ref, local_sem, send_sem, recv_sem, part_send, part_recv, comb_send, comb_recv, mix_send, mix_recv,
):
    me = lax.axis_index("ctx")
    tp = lax.axis_index("tp")
    half = n // 2
    line = me // 2
    side = me % 2
    mate = 2 * line + 1 - side
    rows = kbuf.shape[1]
    width = kbuf.shape[2]
    per = heads // kv_dev
    first_kv = tp * heads // PER
    tokens = n * rows
    pieces = cut.shape[0]
    size = cut.shape[2]
    ndoc = sq_ref.shape[0]

    columns = pl.ds(pl.multiple_of(first_kv * HD, HD), width)
    k_copy = pltpu.make_async_copy(k_hbm.at[:, columns], kbuf.at[me], local_sem.at[0])
    v_copy = pltpu.make_async_copy(v_hbm.at[:, columns], vbuf.at[me], local_sem.at[1])
    q_copy = pltpu.make_async_copy(q_hbm, qbuf, local_sem.at[2])
    w_copy = pltpu.make_async_copy(w_hbm, wbuf, local_sem.at[3])
    k_copy.start()
    v_copy.start()
    small = [
        pltpu.make_async_copy(src, dst, local_sem.at[4 + i])
        for i, (src, dst) in enumerate((
            (doc_hbm, doc_ref), (rep_hbm, rep_ref), (sq_hbm, sq_ref), (sk_hbm, sk_ref), (sv_hbm, sv_ref),
        ))
    ]
    for copy in small:
        copy.start()

    barrier = pltpu.get_barrier_semaphore()
    for t in range(1, n):
        pl.semaphore_signal(barrier, inc=1, device_id={"ctx": lax.rem(me + t, n)}, device_id_type=MESH)
    for t in range(1, ntp):
        pl.semaphore_signal(barrier, inc=1, device_id={"tp": lax.rem(tp + t, ntp)}, device_id_type=MESH)

    pl.semaphore_wait(barrier, (n - 1) + (ntp - 1))

    def move(way, owner, piece):
        buf = (kbuf, vbuf)[piece]
        target = (me + 2, me - 2, mate)[way]
        return pltpu.make_async_remote_copy(
            src_ref=buf.at[owner],
            dst_ref=buf.at[owner],
            send_sem=send_sem.at[way, owner, piece],
            recv_sem=recv_sem.at[owner, piece],
            device_id={"ctx": target},
            device_id_type=MESH,
        )

    def move_own(way, piece):
        target = (me + 2, me - 2, mate)[way]
        return pltpu.make_async_remote_copy(
            src_ref=(k_hbm, v_hbm)[piece].at[:, columns],
            dst_ref=(kbuf, vbuf)[piece].at[me],
            send_sem=send_sem.at[way, me, piece],
            recv_sem=recv_sem.at[me, piece],
            device_id={"ctx": target},
            device_id_type=MESH,
        )

    for piece in range(2):
        @pl.when(line < half - 1)
        def _():
            move_own(0, piece).start()

        @pl.when(line > 0)
        def _():
            move_own(1, piece).start()

        move_own(2, piece).start()
    q_copy.start()
    w_copy.start()

    for copy in small:
        copy.wait()
    docs = doc_ref[...].astype(F32)
    starts = [jnp.sum(jnp.where(docs < d, 1.0, 0.0), axis=1, keepdims=True) for d in range(ndoc + 1)]
    own_docs = doc_ref[:, pl.ds(pl.multiple_of(me * rows, rows), rows)].astype(F32)
    begin = jnp.zeros_like(own_docs)
    for d in range(1, ndoc):
        begin = jnp.where(own_docs == d, starts[d], begin)
    dstart[...] = jnp.transpose(jnp.broadcast_to(begin, (rows, rows)))
    sq_scr[...] = jnp.zeros_like(sq_scr)
    sk_scr[...] = jnp.zeros_like(sk_scr)
    sv_scr[...] = jnp.zeros_like(sv_scr)
    sq = sq_ref[...].astype(F32)
    for h in range(heads):
        low = h % 2 * ndoc
        sq_scr[h // 2, low:low + ndoc, :] = sq[:, h * HD:(h + 1) * HD]
    for g in range(kv_dev):
        head_columns = pl.ds(pl.multiple_of((first_kv + g) * HD, HD), HD)
        for low in (0, ndoc):
            sk_scr[g, low:low + ndoc, :] = sk_ref[:, head_columns].astype(F32)
            sv_scr[g, low:low + ndoc, :] = sv_ref[:, head_columns].astype(F32)
    att[...] = jnp.zeros(att.shape, F32)

    k_copy.wait()
    v_copy.wait()

    pairs = heads // 2
    group_pairs = pairs // kv_dev
    share = pairs // combiners
    shape = (group_pairs * 8, rows)
    row_doc = (lax.broadcasted_iota(jnp.int32, shape, 0) % ndoc).astype(F32)
    inside = row_doc == own_docs
    for g in range(kv_dev):
        lanes = slice(g * HD, (g + 1) * HD)
        q = sq_scr[g * group_pairs:(g + 1) * group_pairs].reshape(group_pairs * 8, HD).astype(BF16)
        s = dot(q, kbuf[me, :, lanes], NT)
        top = jnp.max(jnp.where(inside, s, -1e30), axis=1, keepdims=True)
        weights = jnp.where(inside, jnp.exp2((s - top) * EXP_SCALE), 0.0)
        total = jnp.sum(weights, axis=1, keepdims=True)
        summed = dot(weights.astype(BF16), vbuf[me, :, lanes], NN)
        half_lane = lax.broadcasted_iota(jnp.int32, (group_pairs * 8, HD), 1) < HD // 2
        both = jnp.concatenate([summed, jnp.where(half_lane, top, total)], axis=1)
        part[g * group_pairs:(g + 1) * group_pairs] = both.reshape(group_pairs, 8, 2 * HD)

    def to_combiner(t):
        target = lax.rem(me + t, n)
        return pltpu.make_async_remote_copy(
            src_ref=part.at[pl.ds(jnp.minimum(target, combiners - 1) * share, share)],
            dst_ref=comb.at[me],
            send_sem=comb_send.at[t],
            recv_sem=comb_recv.at[me],
            device_id={"ctx": target},
            device_id_type=MESH,
        )

    def from_device(sender):
        return pltpu.make_async_remote_copy(
            src_ref=comb.at[sender],
            dst_ref=comb.at[sender],
            send_sem=comb_send.at[0],
            recv_sem=comb_recv.at[sender],
            device_id={"ctx": mate},
            device_id_type=MESH,
        )

    def mix_copy(t, slot):
        return pltpu.make_async_remote_copy(
            src_ref=mixed.at[slot],
            dst_ref=mixed.at[slot],
            send_sem=mix_send.at[t],
            recv_sem=mix_recv.at[slot],
            device_id={"ctx": lax.rem(me + t, n)},
            device_id_type=MESH,
        )

    for t in range(1, n):
        @pl.when(lax.rem(me + t, n) < combiners)
        def _():
            to_combiner(t).start()

    tops[...] = jnp.full(tops.shape, -1e30, F32)
    acc[...] = jnp.zeros(acc.shape, F32)

    start = jnp.zeros((1, 1), F32)
    length = jnp.zeros((1, 1), F32)
    for d in range(ndoc):
        named = rep_ref[d] == me
        start = jnp.where(named, starts[d], start)
        length = jnp.where(named, starts[d + 1] - starts[d], length)
    slots = rk_ref.shape[2]
    out_rows = rk_ref.shape[1]
    chunk = slots // max(1, tokens // 1024)
    for first in range(0, slots, chunk):
        slot = (first + lax.broadcasted_iota(jnp.int32, (1, chunk), 1)).astype(F32)
        source = jnp.where(slot < length, slot + start, -1.0)
        position = lax.broadcasted_iota(jnp.int32, (tokens, chunk), 0).astype(F32)
        pick[:, first:first + chunk] = jnp.where(position == source, 1.0, 0.0).astype(BF16)

    def turn(o):
        lanes = pl.ds(pl.multiple_of(2 * o * rows, 2 * rows), 2 * rows)
        kt[:, lanes] = jnp.transpose(kbuf[pl.ds(2 * o, 2)].reshape(2 * rows, width))
        vt[:, lanes] = jnp.transpose(vbuf[pl.ds(2 * o, 2)].reshape(2 * rows, width))

    def combine():
        comb[me] = part[pl.ds(me * share, share)]
        for t in range(1, n):
            from_device(lax.rem(me + t, n)).wait_recv()
        for j in range(share):
            pair = me * share + j
            g = pair // group_pairs
            own = jnp.sum(sq_scr[pair] * sk_scr[g], axis=1, keepdims=True)
            top = own
            for i in range(n):
                top = jnp.maximum(top, comb[i, j, :, HD:HD + 1])
            own_weight = jnp.exp2((own - top) * EXP_SCALE)
            total = own_weight
            summed = own_weight.astype(BF16).astype(F32) * sv_scr[g]
            for i in range(n):
                fade = jnp.exp2((comb[i, j, :, HD:HD + 1] - top) * EXP_SCALE)
                total = total + fade * comb[i, j, :, HD + HD // 2:HD + HD // 2 + 1]
                summed = summed + fade * comb[i, j, :, 0:HD]
            mixed[me, j] = summed / total
        for t in range(1, n):
            mix_copy(t, me).start()

    def project():
        for c in range(combiners):
            @pl.when(c != me)
            def _():
                mix_copy(1, c).wait_recv()
        for h in range(heads):
            low = h % 2 * ndoc
            pair = h // 2
            att[0:ndoc, h * HD:(h + 1) * HD] = mixed[pair // share, pair % share, low:low + ndoc, :]
        w_copy.wait()
        rows_in = att[...].astype(BF16)
        for c in range(pieces):
            cut[c] = dot(rows_in, wbuf[:, c * size:(c + 1) * size], NN)[0:8]
        pack[...] = jnp.zeros_like(pack)
        for c in range(pieces):
            pack[c * ndoc:(c + 1) * ndoc, :] = cut[c, 0:ndoc, :]
        out_buf[...] = pack[...].astype(BF16)
        for t in range(1, ntp):
            term(t).start()

    def term(t):
        return pltpu.make_async_remote_copy(
            src_ref=out_buf,
            dst_ref=in_buf.at[t],
            send_sem=part_send.at[t],
            recv_sem=part_recv.at[t],
            device_id={"tp": lax.rem(tp + t, ntp)},
            device_id_type=MESH,
        )

    def group(o):
        j = 2 * o * rows + lax.broadcasted_iota(jnp.int32, (rows, 2 * rows), 1)
        i = me * rows + lax.broadcasted_iota(jnp.int32, (rows, 2 * rows), 0)
        seen = (j <= i) & (j.astype(F32) >= jnp.concatenate([dstart[...]] * 2, axis=1))
        bias[...] = jnp.where(seen, 0.0, -1e30)
        for g in range(kv_dev):
            lanes = slice(g * HD, (g + 1) * HD)
            k = kbuf[pl.ds(2 * o, 2), :, lanes].reshape(2 * rows, HD)
            v = vbuf[pl.ds(2 * o, 2), :, lanes].reshape(2 * rows, HD)
            v = jnp.concatenate([v, jnp.ones_like(v)], axis=1)

            q = jnp.concatenate(
                [qbuf[:, (g * per + u) * HD:(g * per + u + 1) * HD] for u in range(per)], axis=0
            )
            s = dot(q, k, NT).reshape(per, rows, 2 * rows) + bias[...][None]
            old = tops[g * per:(g + 1) * per]
            top = jnp.maximum(old, jnp.max(s, axis=2, keepdims=True))
            weights = jnp.exp2((s - jnp.concatenate([top, top], axis=2)) * EXP_SCALE)
            fade = jnp.exp2((old - top) * EXP_SCALE)
            tops[g * per:(g + 1) * per] = top
            new = dot(weights.reshape(per * rows, 2 * rows).astype(BF16), v, NN)
            acc[g * per:(g + 1) * per] = (
                acc[g * per:(g + 1) * per] * jnp.concatenate([fade, fade], axis=2)
                + new.reshape(per, rows, 2 * HD)
            )

    results = [
        pltpu.make_async_copy(src, dst, out_sem.at[i])
        for i, (src, dst) in enumerate((
            (ctx_ref, ctx_hbm), (rk_ref, rk_hbm), (rv_ref, rv_hbm), (next_ref, next_hbm),
        ))
    ]
    def finish():
        for h in range(heads):
            ctx_ref[:, h * HD:(h + 1) * HD] = (acc[h, :, 0:HD] / acc[h, :, HD:2 * HD]).astype(BF16)
        results[0].start()

    back = 5 * n // 8
    late = (line >= half - 1) & (2 * (line - half) + 3 >= me - back)

    def step(s, carry):
        low = line - s
        high = line + s
        for piece in range(2):
            @pl.when(low >= 0)
            def _():
                owner = 2 * low + side
                move(0, owner, piece).wait_recv()

                @pl.when(line < half - 1)
                def _():
                    move(0, owner, piece).start()

                move(2, owner, piece).start()

            @pl.when(high < half)
            def _():
                owner = 2 * high + side
                move(1, owner, piece).wait_recv()

                @pl.when(line > 0)
                def _():
                    move(1, owner, piece).start()

                move(2, owner, piece).start()
        @pl.when((s == 1) & (me < combiners))
        def _():
            combine()

        @pl.when(s == half - 1)
        def _():
            project()

        @pl.when((s == half) & jnp.logical_not(late))
        def _():
            finish()

        low = line - (s - 1)
        high = line + (s - 1)

        @pl.when(low >= 0)
        def _():
            for piece in range(2):
                move(2, 2 * low + 1 - side, piece).wait_recv()

        @pl.when((high < half) & (s > 1))
        def _():
            for piece in range(2):
                move(2, 2 * high + 1 - side, piece).wait_recv()

        @pl.when((low >= 0) & (2 * low + 1 >= me - back))
        def _():
            group(low)

        @pl.when((s == half) & late)
        def _():
            finish()

        @pl.when(low >= 0)
        def _():
            turn(low)

        @pl.when((high < half) & (s > 1))
        def _():
            turn(high)

        return carry

    q_copy.wait()
    lax.fori_loop(1, half + 1, step, 0)

    for first in range(0, slots, chunk):
        for turned, ref in ((kt, rk_ref), (vt, rv_ref)):
            taken = dot(turned[...], pick[:, first:first + chunk], NN).astype(BF16)
            if out_rows < width:
                taken = jnp.where(tp % (width // out_rows) == 0, taken[0:out_rows], taken[out_rows:2 * out_rows])
            ref[0, :, first:first + chunk] = taken
    results[1].start()
    results[2].start()

    summed = out_buf[...].astype(F32)
    for t in range(1, ntp):
        term(t).wait_recv()
        summed = summed + in_buf[t].astype(F32)
    replica = lax.broadcasted_iota(jnp.int32, (n, size), 0)
    for c in range(pieces):
        result = jnp.zeros((n, size), F32)
        for d in range(ndoc):
            row = c * ndoc + d
            result = jnp.where(replica == rep_ref[d], summed[row:row + 1, :], result)
        next_ref[:, c * size:(c + 1) * size] = result.astype(BF16)
    results[3].start()
    for t in range(1, ntp):
        term(t).wait_send()
    for t in range(1, n):
        @pl.when(lax.rem(me + t, n) < combiners)
        def _():
            to_combiner(t).wait_send()

        @pl.when(me < combiners)
        def _():
            mix_copy(t, me).wait_send()

    def drain(s, carry):
        for piece in range(2):
            @pl.when(line - s >= 0)
            def _():
                owner = 2 * (line - s) + side

                @pl.when(line < half - 1)
                def _():
                    move(0, owner, piece).wait_send()

                move(2, owner, piece).wait_send()

            @pl.when(line + s < half)
            def _():
                owner = 2 * (line + s) + side

                @pl.when(line > 0)
                def _():
                    move(1, owner, piece).wait_send()

                @pl.when(s > 0)
                def _():
                    move(2, owner, piece).wait_send()
        return carry

    lax.fori_loop(0, half, drain, 0)
    for copy in results:
        copy.wait()


def deliver(*refs):
    inward = [pltpu.make_async_copy(refs[i], refs[8 + i], refs[12].at[i]) for i in range(4)]
    outward = [pltpu.make_async_copy(refs[8 + i], refs[4 + i], refs[12].at[4 + i]) for i in range(4)]
    for copy in inward:
        copy.start()
    for i in range(4):
        inward[i].wait()
        outward[i].start()
    for copy in outward:
        copy.wait()


def local(queries, keys, values, doc_ids, replica_of, step_query, step_key, step_value, out_weight):
    n = lax.axis_size("ctx")
    ntp = lax.axis_size("tp")
    rows, depth = queries.shape
    heads = depth // HD
    kv_dev = max(1, heads // PER)
    tokens = n * rows
    slots = 5 * tokens // 8
    out_columns = out_weight.shape[1]
    width = kv_dev * HD
    pieces = 4 if out_columns % 512 == 0 else 1
    size = out_columns // pieces
    hbm = pl.BlockSpec(memory_space=pl.ANY)
    share = keys.shape[1] // ntp
    pairs = heads // 2
    combiners = max(c for c in range(1, n + 1) if pairs % c == 0)
    results = pl.pallas_call(
        functools.partial(kernel, n, ntp, heads, kv_dev, combiners),
        out_shape=(
            jax.ShapeDtypeStruct((rows, depth), BF16),
            jax.ShapeDtypeStruct((n, out_columns), BF16),
            jax.ShapeDtypeStruct((1, share, slots), BF16),
            jax.ShapeDtypeStruct((1, share, slots), BF16),
        ),
        in_specs=[hbm] * 9,
        out_specs=(hbm,) * 4,
        scratch_shapes=[
            pltpu.VMEM((n, rows, width), BF16),
            pltpu.VMEM((n, rows, width), BF16),
            pltpu.VMEM((rows, depth), BF16),
            pltpu.VMEM((depth, out_columns), BF16),
            pltpu.VMEM((heads, rows, 2 * HD), F32),
            pltpu.VMEM((heads, rows, HD), F32),
            pltpu.VMEM((rows, 2 * rows), F32),
            pltpu.VMEM((rows, rows), F32),
            pltpu.VMEM((pairs, 8, HD), F32),
            pltpu.VMEM((kv_dev, 8, HD), F32),
            pltpu.VMEM((kv_dev, 8, HD), F32),
            pltpu.VMEM((16, depth), F32),
            pltpu.VMEM((16, size), F32),
            pltpu.VMEM((pieces, 8, size), F32),
            pltpu.VMEM((16, size), BF16),
            pltpu.VMEM((ntp, 16, size), BF16),
            pltpu.VMEM((pairs, 8, 2 * HD), F32),
            pltpu.VMEM((n, pairs // combiners, 8, 2 * HD), F32),
            pltpu.VMEM((combiners, pairs // combiners, 8, HD), F32),
            pltpu.VMEM((tokens, slots), BF16),
            pltpu.VMEM((width, tokens), BF16),
            pltpu.VMEM((width, tokens), BF16),
            pltpu.VMEM((rows, depth), BF16),
            pltpu.VMEM((n, out_columns), BF16),
            pltpu.VMEM((1, share, slots), BF16),
            pltpu.VMEM((1, share, slots), BF16),
            pltpu.SemaphoreType.DMA((4,)),
            pltpu.VMEM((1, tokens), jnp.int32),
            pltpu.SMEM(replica_of.shape, jnp.int32),
            pltpu.VMEM(step_query.shape, BF16),
            pltpu.VMEM(step_key.shape, BF16),
            pltpu.VMEM(step_value.shape, BF16),
            pltpu.SemaphoreType.DMA((9,)),
            pltpu.SemaphoreType.DMA((3, n, 2)),
            pltpu.SemaphoreType.DMA((n, 2)),
            pltpu.SemaphoreType.DMA((ntp,)),
            pltpu.SemaphoreType.DMA((ntp,)),
            pltpu.SemaphoreType.DMA((n,)),
            pltpu.SemaphoreType.DMA((n,)),
            pltpu.SemaphoreType.DMA((n,)),
            pltpu.SemaphoreType.DMA((n,)),
        ],
        compiler_params=pltpu.CompilerParams(
            collective_id=0, has_side_effects=True, vmem_limit_bytes=60 * 1024 * 1024
        ),
    )(queries, keys, values, doc_ids.reshape(1, tokens), replica_of, step_query, step_key, step_value, out_weight)
    return pl.pallas_call(
        deliver,
        out_shape=tuple(jax.ShapeDtypeStruct(r.shape, r.dtype) for r in results),
        in_specs=[hbm] * 4,
        out_specs=(hbm,) * 4,
        scratch_shapes=[pltpu.VMEM(r.shape, r.dtype) for r in results] + [pltpu.SemaphoreType.DMA((8,))],
        compiler_params=pltpu.CompilerParams(vmem_limit_bytes=60 * 1024 * 1024),
    )(*results)


def solution(mesh):
    placed = (
        P("ctx", "tp"),
        P("ctx", None),
        P("ctx", None),
        P(),
        P(),
        P(None, "tp"),
        P(),
        P(),
        P("tp", "ctx"),
    )
    return jax.shard_map(
        local,
        mesh=mesh,
        in_specs=placed,
        out_specs=(P("ctx", "tp"), P(None, "ctx"), P("ctx", "tp", None), P("ctx", "tp", None)),
        check_vma=False,
    )
```

```python
import functools
import math

import jax
import jax.numpy as jnp
from jax import lax
from jax.experimental import pallas as pl
from jax.experimental.pallas import tpu as pltpu
from jax.sharding import PartitionSpec as P

H = 96
KVH = 8
HD = 128
PER = H // KVH
MESH = pl.DeviceIdType.MESH
EXP_SCALE = math.log2(math.e) / math.sqrt(HD)
F32 = jnp.float32
BF16 = jnp.bfloat16
NT = (((1,), (1,)), ((), ()))
NN = (((1,), (0,)), ((), ()))
TN = (((0,), (0,)), ((), ()))


def dot(a, b, dims):
    return lax.dot_general(a, b, dims, preferred_element_type=F32)


def kernel(
    n, ntp, heads, kv_dev,
    q_hbm, k_hbm, v_hbm, doc_hbm, rep_hbm, sq_hbm, sk_hbm, sv_hbm, w_hbm,
    ctx_hbm, next_hbm, rk_hbm, rv_hbm,
    kbuf, vbuf, qbuf, wbuf, acc, tops, bias, dstart, sq_scr, sk_scr, sv_scr, att, pack, cut, out_buf, in_buf,
    mixed, ctx_ref, next_ref, rk_ref, rv_ref, out_sem,
    doc_ref, rep_ref, sq_ref, sk_ref, sv_ref, local_sem, send_sem, recv_sem, part_send, part_recv,
):
    me = lax.axis_index("ctx")
    tp = lax.axis_index("tp")
    half = n // 2
    line = me // 2
    side = me % 2
    mate = 2 * line + 1 - side
    rows = kbuf.shape[1]
    width = kbuf.shape[2]
    per = heads // kv_dev
    first_kv = tp * heads // PER
    tokens = n * rows
    pieces = cut.shape[0]
    size = cut.shape[2]
    ndoc = sq_ref.shape[0]

    columns = pl.ds(pl.multiple_of(first_kv * HD, HD), width)
    k_copy = pltpu.make_async_copy(k_hbm.at[:, columns], kbuf.at[me], local_sem.at[0])
    v_copy = pltpu.make_async_copy(v_hbm.at[:, columns], vbuf.at[me], local_sem.at[1])
    q_copy = pltpu.make_async_copy(q_hbm, qbuf, local_sem.at[2])
    w_copy = pltpu.make_async_copy(w_hbm, wbuf, local_sem.at[3])
    k_copy.start()
    v_copy.start()
    small = [
        pltpu.make_async_copy(src, dst, local_sem.at[4 + i])
        for i, (src, dst) in enumerate((
            (doc_hbm, doc_ref), (rep_hbm, rep_ref), (sq_hbm, sq_ref), (sk_hbm, sk_ref), (sv_hbm, sv_ref),
        ))
    ]
    for copy in small:
        copy.start()

    barrier = pltpu.get_barrier_semaphore()
    for t in range(1, n):
        pl.semaphore_signal(barrier, inc=1, device_id={"ctx": lax.rem(me + t, n)}, device_id_type=MESH)
    for t in range(1, ntp):
        pl.semaphore_signal(barrier, inc=1, device_id={"tp": lax.rem(tp + t, ntp)}, device_id_type=MESH)

    pl.semaphore_wait(barrier, (n - 1) + (ntp - 1))

    def move(way, owner, piece):
        buf = (kbuf, vbuf)[piece]
        target = (me + 2, me - 2, mate)[way]
        return pltpu.make_async_remote_copy(
            src_ref=buf.at[owner],
            dst_ref=buf.at[owner],
            send_sem=send_sem.at[way, owner, piece],
            recv_sem=recv_sem.at[owner, piece],
            device_id={"ctx": target},
            device_id_type=MESH,
        )

    def move_own(way, piece):
        target = (me + 2, me - 2, mate)[way]
        return pltpu.make_async_remote_copy(
            src_ref=(k_hbm, v_hbm)[piece].at[:, columns],
            dst_ref=(kbuf, vbuf)[piece].at[me],
            send_sem=send_sem.at[way, me, piece],
            recv_sem=recv_sem.at[me, piece],
            device_id={"ctx": target},
            device_id_type=MESH,
        )

    for piece in range(2):
        @pl.when(line < half - 1)
        def _():
            move_own(0, piece).start()

        @pl.when(line > 0)
        def _():
            move_own(1, piece).start()

        move_own(2, piece).start()
    q_copy.start()
    w_copy.start()

    for copy in small:
        copy.wait()
    docs = doc_ref[...].astype(F32)
    starts = [jnp.sum(jnp.where(docs < d, 1.0, 0.0), axis=1, keepdims=True) for d in range(ndoc + 1)]
    own_docs = doc_ref[:, pl.ds(pl.multiple_of(me * rows, rows), rows)].astype(F32)
    begin = jnp.zeros_like(own_docs)
    for d in range(1, ndoc):
        begin = jnp.where(own_docs == d, starts[d], begin)
    dstart[...] = jnp.transpose(jnp.broadcast_to(begin, (rows, rows)))
    sq_scr[...] = jnp.zeros_like(sq_scr)
    sk_scr[...] = jnp.zeros_like(sk_scr)
    sv_scr[...] = jnp.zeros_like(sv_scr)
    sq = sq_ref[...].astype(F32)
    for h in range(heads):
        low = h % 2 * ndoc
        sq_scr[h // 2, low:low + ndoc, :] = sq[:, h * HD:(h + 1) * HD]
    for g in range(kv_dev):
        head_columns = pl.ds(pl.multiple_of((first_kv + g) * HD, HD), HD)
        for low in (0, ndoc):
            sk_scr[g, low:low + ndoc, :] = sk_ref[:, head_columns].astype(F32)
            sv_scr[g, low:low + ndoc, :] = sv_ref[:, head_columns].astype(F32)
    att[...] = jnp.zeros(att.shape, F32)

    k_copy.wait()
    v_copy.wait()

    pairs = heads // 2
    group_pairs = pairs // kv_dev
    tops[...] = jnp.full(tops.shape, -1e30, F32)
    acc[...] = jnp.zeros(acc.shape, F32)

    def decode():
        shape = (group_pairs * 8, tokens)
        row_doc = (lax.broadcasted_iota(jnp.int32, shape, 0) % ndoc).astype(F32)
        inside = row_doc == docs
        for g in range(kv_dev):
            lanes = slice(g * HD, (g + 1) * HD)
            q = sq_scr[g * group_pairs:(g + 1) * group_pairs]
            own = jnp.sum(q * sk_scr[g][None], axis=2, keepdims=True).reshape(group_pairs * 8, 1)
            q = q.reshape(group_pairs * 8, HD).astype(BF16)
            s = dot(q, kbuf[:, :, lanes].reshape(tokens, HD), NT)
            top = jnp.maximum(jnp.max(jnp.where(inside, s, -1e30), axis=1, keepdims=True), own)
            weights = jnp.where(inside, jnp.exp2((s - top) * EXP_SCALE), 0.0)
            own_weight = jnp.exp2((own - top) * EXP_SCALE)
            total = jnp.sum(weights, axis=1, keepdims=True) + own_weight
            own_value = jnp.broadcast_to(sv_scr[g][None], (group_pairs, 8, HD)).reshape(group_pairs * 8, HD)
            summed = dot(weights.astype(BF16), vbuf[:, :, lanes].reshape(tokens, HD), NN)
            summed = (summed + own_weight.astype(BF16).astype(F32) * own_value) / total
            mixed[g * group_pairs:(g + 1) * group_pairs] = summed.reshape(group_pairs, 8, HD)

    def project():
        for h in range(heads):
            low = h % 2 * ndoc
            pair = h // 2
            att[0:ndoc, h * HD:(h + 1) * HD] = mixed[pair, low:low + ndoc, :]
        w_copy.wait()
        rows_in = att[...].astype(BF16)
        for c in range(pieces):
            cut[c] = dot(rows_in, wbuf[:, c * size:(c + 1) * size], NN)[0:8]
        pack[...] = jnp.zeros_like(pack)
        for c in range(pieces):
            pack[c * ndoc:(c + 1) * ndoc, :] = cut[c, 0:ndoc, :]
        out_buf[...] = pack[...].astype(BF16)
        for t in range(1, ntp):
            term(t).start()

    def term(t):
        return pltpu.make_async_remote_copy(
            src_ref=out_buf,
            dst_ref=in_buf.at[t],
            send_sem=part_send.at[t],
            recv_sem=part_recv.at[t],
            device_id={"tp": lax.rem(tp + t, ntp)},
            device_id_type=MESH,
        )

    def group(o):
        j = 2 * o * rows + lax.broadcasted_iota(jnp.int32, (rows, 2 * rows), 1)
        i = me * rows + lax.broadcasted_iota(jnp.int32, (rows, 2 * rows), 0)
        seen = (j <= i) & (j.astype(F32) >= jnp.concatenate([dstart[...]] * 2, axis=1))
        bias[...] = jnp.where(seen, 0.0, -1e30)
        for g in range(kv_dev):
            lanes = slice(g * HD, (g + 1) * HD)
            k = kbuf[pl.ds(2 * o, 2), :, lanes].reshape(2 * rows, HD)
            v = vbuf[pl.ds(2 * o, 2), :, lanes].reshape(2 * rows, HD)
            v = jnp.concatenate([v, jnp.ones_like(v)], axis=1)

            q = jnp.concatenate(
                [qbuf[:, (g * per + u) * HD:(g * per + u + 1) * HD] for u in range(per)], axis=0
            )
            s = dot(q, k, NT).reshape(per, rows, 2 * rows) + bias[...][None]
            old = tops[g * per:(g + 1) * per]
            top = jnp.maximum(old, jnp.max(s, axis=2, keepdims=True))
            weights = jnp.exp2((s - jnp.concatenate([top, top], axis=2)) * EXP_SCALE)
            fade = jnp.exp2((old - top) * EXP_SCALE)
            tops[g * per:(g + 1) * per] = top
            new = dot(weights.reshape(per * rows, 2 * rows).astype(BF16), v, NN)
            acc[g * per:(g + 1) * per] = (
                acc[g * per:(g + 1) * per] * jnp.concatenate([fade, fade], axis=2)
                + new.reshape(per, rows, 2 * HD)
            )

    results = [
        pltpu.make_async_copy(src, dst, out_sem.at[i])
        for i, (src, dst) in enumerate((
            (ctx_ref, ctx_hbm), (rk_ref, rk_hbm), (rv_ref, rv_hbm), (next_ref, next_hbm),
        ))
    ]
    def finish():
        for h in range(heads):
            ctx_ref[:, h * HD:(h + 1) * HD] = (acc[h, :, 0:HD] / acc[h, :, HD:2 * HD]).astype(BF16)
        results[0].start()

    back = 5 * n // 8
    late = (line >= half - 1) & (2 * (line - half) + 3 >= me - back)

    def step(s, carry):
        low = line - s
        high = line + s
        for piece in range(2):
            @pl.when(low >= 0)
            def _():
                owner = 2 * low + side
                move(0, owner, piece).wait_recv()

                @pl.when(line < half - 1)
                def _():
                    move(0, owner, piece).start()

                move(2, owner, piece).start()

            @pl.when(high < half)
            def _():
                owner = 2 * high + side
                move(1, owner, piece).wait_recv()

                @pl.when(line > 0)
                def _():
                    move(1, owner, piece).start()

                move(2, owner, piece).start()
        @pl.when((s == half) & jnp.logical_not(late))
        def _():
            finish()

        low = line - (s - 1)
        high = line + (s - 1)

        @pl.when(low >= 0)
        def _():
            for piece in range(2):
                move(2, 2 * low + 1 - side, piece).wait_recv()

        @pl.when((high < half) & (s > 1))
        def _():
            for piece in range(2):
                move(2, 2 * high + 1 - side, piece).wait_recv()

        @pl.when((low >= 0) & (2 * low + 1 >= me - back))
        def _():
            group(low)

        @pl.when((s == half) & late)
        def _():
            finish()

        return carry

    q_copy.wait()
    lax.fori_loop(1, half + 1, step, 0)
    decode()
    project()

    start = jnp.zeros((1, 1), F32)
    length = jnp.zeros((1, 1), F32)
    for d in range(ndoc):
        named = rep_ref[d] == me
        start = jnp.where(named, starts[d], start)
        length = jnp.where(named, starts[d + 1] - starts[d], length)
    slots = rk_ref.shape[2]
    out_rows = rk_ref.shape[1]
    chunk = slots // max(1, tokens // 1024)
    for first in range(0, slots, chunk):
        slot = (first + lax.broadcasted_iota(jnp.int32, (1, chunk), 1)).astype(F32)
        source = jnp.where(slot < length, slot + start, -1.0)
        position = lax.broadcasted_iota(jnp.int32, (tokens, chunk), 0).astype(F32)
        pick = jnp.where(position == source, 1.0, 0.0).astype(BF16)
        for buf, ref in ((kbuf, rk_ref), (vbuf, rv_ref)):
            taken = dot(buf[...].reshape(tokens, width), pick, TN).astype(BF16)
            if out_rows < width:
                taken = jnp.where(tp % (width // out_rows) == 0, taken[0:out_rows], taken[out_rows:2 * out_rows])
            ref[0, :, first:first + chunk] = taken

    results[1].start()
    results[2].start()

    summed = out_buf[...].astype(F32)
    for t in range(1, ntp):
        term(t).wait_recv()
        summed = summed + in_buf[t].astype(F32)
    replica = lax.broadcasted_iota(jnp.int32, (n, size), 0)
    for c in range(pieces):
        result = jnp.zeros((n, size), F32)
        for d in range(ndoc):
            row = c * ndoc + d
            result = jnp.where(replica == rep_ref[d], summed[row:row + 1, :], result)
        next_ref[:, c * size:(c + 1) * size] = result.astype(BF16)
    results[3].start()
    for t in range(1, ntp):
        term(t).wait_send()
    def drain(s, carry):
        for piece in range(2):
            @pl.when(line - s >= 0)
            def _():
                owner = 2 * (line - s) + side

                @pl.when(line < half - 1)
                def _():
                    move(0, owner, piece).wait_send()

                move(2, owner, piece).wait_send()

            @pl.when(line + s < half)
            def _():
                owner = 2 * (line + s) + side

                @pl.when(line > 0)
                def _():
                    move(1, owner, piece).wait_send()

                @pl.when(s > 0)
                def _():
                    move(2, owner, piece).wait_send()
        return carry

    lax.fori_loop(0, half, drain, 0)
    for copy in results:
        copy.wait()


def deliver(*refs):
    inward = [pltpu.make_async_copy(refs[i], refs[8 + i], refs[12].at[i]) for i in range(4)]
    outward = [pltpu.make_async_copy(refs[8 + i], refs[4 + i], refs[12].at[4 + i]) for i in range(4)]
    for copy in inward:
        copy.start()
    for i in range(4):
        inward[i].wait()
        outward[i].start()
    for copy in outward:
        copy.wait()


def local(queries, keys, values, doc_ids, replica_of, step_query, step_key, step_value, out_weight):
    n = lax.axis_size("ctx")
    ntp = lax.axis_size("tp")
    rows, depth = queries.shape
    heads = depth // HD
    kv_dev = max(1, heads // PER)
    tokens = n * rows
    slots = 5 * tokens // 8
    out_columns = out_weight.shape[1]
    width = kv_dev * HD
    pieces = 4 if out_columns % 512 == 0 else 1
    size = out_columns // pieces
    hbm = pl.BlockSpec(memory_space=pl.ANY)
    share = keys.shape[1] // ntp
    pairs = heads // 2
    results = pl.pallas_call(
        functools.partial(kernel, n, ntp, heads, kv_dev),
        out_shape=(
            jax.ShapeDtypeStruct((rows, depth), BF16),
            jax.ShapeDtypeStruct((n, out_columns), BF16),
            jax.ShapeDtypeStruct((1, share, slots), BF16),
            jax.ShapeDtypeStruct((1, share, slots), BF16),
        ),
        in_specs=[hbm] * 9,
        out_specs=(hbm,) * 4,
        scratch_shapes=[
            pltpu.VMEM((n, rows, width), BF16),
            pltpu.VMEM((n, rows, width), BF16),
            pltpu.VMEM((rows, depth), BF16),
            pltpu.VMEM((depth, out_columns), BF16),
            pltpu.VMEM((heads, rows, 2 * HD), F32),
            pltpu.VMEM((heads, rows, HD), F32),
            pltpu.VMEM((rows, 2 * rows), F32),
            pltpu.VMEM((rows, rows), F32),
            pltpu.VMEM((pairs, 8, HD), F32),
            pltpu.VMEM((kv_dev, 8, HD), F32),
            pltpu.VMEM((kv_dev, 8, HD), F32),
            pltpu.VMEM((16, depth), F32),
            pltpu.VMEM((16, size), F32),
            pltpu.VMEM((pieces, 8, size), F32),
            pltpu.VMEM((16, size), BF16),
            pltpu.VMEM((ntp, 16, size), BF16),
            pltpu.VMEM((pairs, 8, HD), F32),
            pltpu.VMEM((rows, depth), BF16),
            pltpu.VMEM((n, out_columns), BF16),
            pltpu.VMEM((1, share, slots), BF16),
            pltpu.VMEM((1, share, slots), BF16),
            pltpu.SemaphoreType.DMA((4,)),
            pltpu.VMEM((1, tokens), jnp.int32),
            pltpu.SMEM(replica_of.shape, jnp.int32),
            pltpu.VMEM(step_query.shape, BF16),
            pltpu.VMEM(step_key.shape, BF16),
            pltpu.VMEM(step_value.shape, BF16),
            pltpu.SemaphoreType.DMA((9,)),
            pltpu.SemaphoreType.DMA((3, n, 2)),
            pltpu.SemaphoreType.DMA((n, 2)),
            pltpu.SemaphoreType.DMA((ntp,)),
            pltpu.SemaphoreType.DMA((ntp,)),
        ],
        compiler_params=pltpu.CompilerParams(
            collective_id=0, has_side_effects=True, vmem_limit_bytes=60 * 1024 * 1024
        ),
    )(queries, keys, values, doc_ids.reshape(1, tokens), replica_of, step_query, step_key, step_value, out_weight)
    return pl.pallas_call(
        deliver,
        out_shape=tuple(jax.ShapeDtypeStruct(r.shape, r.dtype) for r in results),
        in_specs=[hbm] * 4,
        out_specs=(hbm,) * 4,
        scratch_shapes=[pltpu.VMEM(r.shape, r.dtype) for r in results] + [pltpu.SemaphoreType.DMA((8,))],
        compiler_params=pltpu.CompilerParams(vmem_limit_bytes=60 * 1024 * 1024),
    )(*results)


def solution(mesh):
    placed = (
        P("ctx", "tp"),
        P("ctx", None),
        P("ctx", None),
        P(),
        P(),
        P(None, "tp"),
        P(),
        P(),
        P("tp", "ctx"),
    )
    return jax.shard_map(
        local,
        mesh=mesh,
        in_specs=placed,
        out_specs=(P("ctx", "tp"), P(None, "ctx"), P("ctx", "tp", None), P("ctx", "tp", None)),
        check_vma=False,
    )
```
